256 devices in a mesh: group: 8 (over y_lo, x), blk: 32 (over z, y_hi, core).
Axes of the slice: x: 4, y: 4 (y_hi: 2, y_lo: 2; y = y_hi * 2 + y_lo), z: 8, core: 2. Of those that a mesh axis runs over, the one named last changes fastest.
Arguments:
- candidates: bfloat16 [32768, 8, 4096], P('blk', 'group'), may hold values from -6 to 6
- queries: bfloat16 [1024, 8, 4096], P('blk', 'group'), may hold values from -6 to 6
- out_factor: float32 [8, 64, 64], P('group'), may hold values from -0.75 to 0.75
- in_factor: float32 [8, 64, 64], P('group'), may hold values from -0.75 to 0.75
- panel_order: int32 [32], replicated, may hold values from 0 to 31, each once
Outputs:
- scores: float32 [32768, 1024], P('blk', 'group')
The draws below stay inside these ranges and needn't reach their ends.
Inputs may be any that keep to these rules, and one draw needn't show every extreme that they name: `panel_order`: a permutation of the panel numbers.
All inputs are finite; a program needn't handle non-finite values.
Results may differ from the reference program's by a relative error of at most 0.0029.
Values may be sent and summed in bfloat16 or wider, within the bound.
No kernel may reach another device: no remote copies, remote signals or barrier semaphores. Data moves between devices by JAX's collectives and lax.ppermute only.
A program may use at most 64 MiB of HBM per device.

```python
import jax
import jax.numpy as jnp
from jax import lax

KO = 64
KI = 64
F = 4096
LAYERS = 8
QPAN = 32
CANDIDATES = 32768
QUERIES = 1024
N_BLK = 32


def block_levels(key, dims, pieces, low, largest):
    loudness = 1.0
    for position, blocks in pieces:
        steps = jax.random.uniform(jax.random.fold_in(jax.random.fold_in(key, 6), position), (blocks,), jnp.float32, low / len(pieces), largest / len(pieces))
        loudness = loudness * jnp.repeat(jnp.exp(steps), dims[position] // blocks).reshape((-1,) + (1,) * (len(dims) - 1 - position))
    return loudness


def scatter_about(key, shape, scale, limit, cuts=(), dtype=jnp.bfloat16):
    result = scale * jax.random.normal(key, shape, jnp.float32)
    if cuts:
        result = result * block_levels(key, shape, cuts, -0.22, 0.18)
    return jnp.clip(result, -limit, limit).astype(dtype)


def setup_inputs(seed: int = 0) -> dict:
    key_list = jax.random.split(jax.random.key(seed), 6)
    return {
        "candidates": scatter_about(key_list[0], (CANDIDATES, LAYERS, F), 1.0, 6.0, ((0, 32), (1, 8))),
        "queries": scatter_about(key_list[1], (QUERIES, LAYERS, F), 1.0, 6.0, ((0, 32), (1, 8))),
        "out_factor": scatter_about(key_list[2], (LAYERS, KO, KO), KO ** -0.5, 0.75, ((0, 8),), jnp.float32),
        "in_factor": scatter_about(key_list[3], (LAYERS, KI, KI), KI ** -0.5, 0.75, ((0, 8),), jnp.float32),
        "panel_order": jax.random.permutation(key_list[4], N_BLK).astype(jnp.int32),
    }


def reference(candidates, queries, out_factor, in_factor, panel_order):
    grads = queries.astype(jnp.float32).reshape(QUERIES, LAYERS, KO, KI)
    left = jnp.einsum("lab,qlbc->qlac", out_factor, grads, precision=lax.Precision.HIGHEST)
    precond = jnp.einsum("qlac,lcd->qlad", left, in_factor, precision=lax.Precision.HIGHEST)
    precond = precond.reshape(QUERIES, LAYERS * F).astype(jnp.bfloat16)
    flat = candidates.reshape(CANDIDATES, LAYERS * F)
    raw = lax.dot_general(flat, precond, (((1,), (1,)), ((), ())), preferred_element_type=jnp.float32)
    raw = raw * (1.0 / (F * LAYERS) ** 0.5)
    ordered = raw.reshape(CANDIDATES, N_BLK, QPAN)[:, panel_order.astype(jnp.int32), :]
    return ordered.reshape(CANDIDATES, QUERIES)
```

```python
import functools

import jax
import jax.numpy as jnp
from jax import lax
from jax.experimental import pallas as pl
from jax.experimental.pallas import tpu as pltpu
from jax.sharding import PartitionSpec as P

NZ = 8
PANEL = 32
CBLK = 256


def _move(x, dz=0, flip_y=False, flip_core=False):
    route = []
    for i in range(NZ * 4):
        z, rest = divmod(i, 4)
        route.append((i, ((z + dz) % NZ) * 4 + (rest ^ (2 * flip_y) ^ (1 * flip_core))))
    return lax.ppermute(x, "blk", route)


def _score_kernel(scale, count, *refs):
    c_ref, o_ref = refs[count], refs[count + 1]
    panels = jnp.concatenate([r[...] for r in refs[:count]], axis=0)
    part = lax.dot_general(
        panels, c_ref[...], (((1,), (1,)), ((), ())), preferred_element_type=jnp.float32
    )
    o_ref[...] = (part * scale).astype(o_ref.dtype)


def _score(pieces, flat, scale):
    rows, feats = flat.shape
    n = sum(p.shape[0] for p in pieces)
    return pl.pallas_call(
        functools.partial(_score_kernel, scale, len(pieces)),
        grid=(rows // CBLK,),
        in_specs=[pl.BlockSpec(p.shape, lambda i: (0, 0)) for p in pieces]
        + [pl.BlockSpec((CBLK, feats), lambda i: (i, 0))],
        out_specs=pl.BlockSpec((n, CBLK), lambda i: (0, i)),
        out_shape=jax.ShapeDtypeStruct((n, rows), jnp.bfloat16),
        compiler_params=pltpu.CompilerParams(vmem_limit_bytes=24 << 20),
        cost_estimate=pl.CostEstimate(
            flops=2 * n * rows * feats, bytes_accessed=2 * (rows * feats + n * feats + n * rows), transcendentals=0
        ),
        name="score",
    )(*pieces, flat)


def _place_kernel(counts, where_ref, *refs):
    out = refs[-1]
    slot = 0
    for ref, count in zip(refs[:-1], counts):
        for i in range(count):
            out[where_ref[slot]] = ref[i * PANEL : (i + 1) * PANEL, :]
            slot += 1


def _place(parts, where):
    counts = [p.shape[0] // PANEL for p in parts]
    rows = parts[0].shape[1]
    return pl.pallas_call(
        functools.partial(_place_kernel, counts),
        in_specs=[pl.BlockSpec(memory_space=pltpu.SMEM)]
        + [pl.BlockSpec(memory_space=pltpu.VMEM) for _ in parts],
        out_specs=pl.BlockSpec(memory_space=pltpu.VMEM),
        out_shape=jax.ShapeDtypeStruct((sum(counts), PANEL, rows), jnp.bfloat16),
        compiler_params=pltpu.CompilerParams(vmem_limit_bytes=16 << 20),
        name="place",
    )(where, *parts)


def _total_kernel(in_ref, o_ref):
    total = in_ref[0].astype(jnp.float32)
    for g in range(1, in_ref.shape[0]):
        total += in_ref[g].astype(jnp.float32)
    o_ref[...] = total.T


def _total(parts):
    groups, width, rows = parts.shape
    return pl.pallas_call(
        _total_kernel,
        grid=(rows // CBLK,),
        in_specs=[pl.BlockSpec((groups, width, CBLK), lambda i: (0, 0, i))],
        out_specs=pl.BlockSpec((CBLK, width), lambda i: (i, 0)),
        out_shape=jax.ShapeDtypeStruct((rows, width), jnp.float32),
        compiler_params=pltpu.CompilerParams(vmem_limit_bytes=16 << 20),
        name="total",
    )(parts)


def body(candidates, queries, out_factor, in_factor, panel_order):
    cand_rows, layer_count, features = candidates.shape
    width = queries.shape[0]
    out_units = out_factor.shape[1]
    in_units = in_factor.shape[1]
    groups = lax.axis_size("group")
    scale = 1.0 / (features * layer_count * groups) ** 0.5
    grads = queries.astype(jnp.float32).reshape(width, layer_count, out_units, in_units)
    left = jnp.einsum("lab,qlbc->qlac", out_factor, grads, precision=lax.Precision.HIGHEST)
    precond = jnp.einsum("qlac,lcd->qlad", left, in_factor, precision=lax.Precision.HIGHEST)
    panel = precond.reshape(width, layer_count * features).astype(jnp.bfloat16)
    flat = candidates.reshape(cand_rows, layer_count * features)

    slots = []

    own = jnp.concatenate([panel, _move(panel, flip_y=True)], axis=0)
    steps = []

    def meet(arrivals):
        pieces = [a for a, _ in arrivals]
        pieces += [_move(a, flip_core=True) for a, _ in arrivals]
        for dc in (0, 1):
            for _, where in arrivals:
                slots.extend((dz, dy, dc) for dz, dy in where)
        steps.append(_score(pieces, flat, scale))

    meet([(own, [(0, 0), (0, 1)])])
    fw = bw = own
    for s in range(1, NZ // 2):
        fw, bw = _move(fw, dz=1), _move(bw, dz=-1)
        meet([(fw, [(-s, 0), (-s, 1)]), (bw, [(s, 0), (s, 1)])])
    s = NZ // 2
    last_fw, last_bw = _move(fw[:PANEL], dz=1), _move(bw[PANEL:], dz=-1)
    meet([(last_fw, [(-s, 0)]), (last_bw, [(s, 1)])])

    me = lax.axis_index("blk")
    z, rest = me // 4, me % 4
    dz = jnp.array([t[0] for t in slots], jnp.int32)
    flip = jnp.array([t[1] * 2 + t[2] for t in slots], jnp.int32)
    source = ((z + dz) % NZ) * 4 + (rest ^ flip)
    places = jnp.arange(panel_order.shape[0], dtype=jnp.int32)
    where = jnp.sum(jnp.where(panel_order[None, :] == source[:, None], places[None, :], 0), axis=1).astype(jnp.int32)
    buffer = _place(steps, where).reshape(groups, -1, cand_rows)
    parts = lax.all_to_all(buffer, "group", split_axis=0, concat_axis=0, tiled=True)
    return _total(parts)


def solution(mesh):
    in_specs = (
        P("blk", "group", None),
        P("blk", "group", None),
        P("group", None, None),
        P("group", None, None),
        P(),
    )
    out_specs = P("blk", "group")
    return jax.shard_map(body, mesh=mesh, in_specs=in_specs, out_specs=out_specs, check_vma=False)
```

```python
import functools

import jax
import jax.numpy as jnp
from jax import lax
from jax.experimental import pallas as pl
from jax.experimental.pallas import tpu as pltpu
from jax.sharding import PartitionSpec as P

NZ = 8
NX = 4
NG = 8
PANEL = 32


def _move(x, dz=0, flip_y=False, flip_core=False):
    route = []
    for i in range(NZ * 4):
        z, rest = divmod(i, 4)
        route.append((i, ((z + dz) % NZ) * 4 + (rest ^ (2 * flip_y) ^ (1 * flip_core))))
    return lax.ppermute(x, "blk", route)


def _group_move(x, dx):
    route = []
    for i in range(NG):
        y, xi = divmod(i, NX)
        route.append((i, y * NX + (xi + dx) % NX))
    return lax.ppermute(x, "group", route)


def _score_kernel(scale, count, x_ref, *refs):
    c_ref, outs = refs[count], refs[count + 1 :]
    panels = jnp.concatenate([r[...] for r in refs[:count]], axis=0)
    part = lax.dot_general(
        panels, c_ref[...], (((1,), (1,)), ((), ())), preferred_element_type=jnp.float32
    )
    part = part * scale
    step = pl.program_id(0)
    for d, out in enumerate(outs):

        @pl.when(step == d)
        def _():
            out[...] = part.astype(out.dtype)


def _score(x_index, pieces, flat, scale):
    rows, feats = flat.shape
    n = sum(p.shape[0] for p in pieces)
    cut = rows // NX
    return pl.pallas_call(
        functools.partial(_score_kernel, scale, len(pieces)),
        grid_spec=pltpu.PrefetchScalarGridSpec(
            num_scalar_prefetch=1,
            grid=(NX,),
            in_specs=[pl.BlockSpec(p.shape, lambda i, x: (0, 0)) for p in pieces]
            + [pl.BlockSpec((cut, feats), lambda i, x: (lax.rem(x[0] + i, NX), 0))],
            out_specs=[pl.BlockSpec((n, cut), lambda i, x: (0, 0)) for _ in range(NX)],
        ),
        out_shape=[
            jax.ShapeDtypeStruct((n, cut), jnp.bfloat16 if d else jnp.float32) for d in range(NX)
        ],
        compiler_params=pltpu.CompilerParams(vmem_limit_bytes=24 << 20),
        cost_estimate=pl.CostEstimate(
            flops=2 * n * rows * feats, bytes_accessed=2 * (rows * feats + n * feats + n * rows), transcendentals=0
        ),
        name="score",
    )(x_index, *pieces, flat)


def _place_kernel(counts, where_ref, *refs):
    out = refs[-1]
    slot = 0
    for s, count in enumerate(counts):
        own, *others = refs[NX * s : NX * s + NX]
        for i in range(count):
            rows = slice(i * PANEL, (i + 1) * PANEL)
            total = own[rows, :]
            for r in others:
                total += r[rows, :].astype(jnp.float32)
            out[where_ref[slot]] = total.astype(out.dtype)
            slot += 1


def _place(parts, where):
    counts = [p[0].shape[0] // PANEL for p in parts]
    cut = parts[0][0].shape[1]
    flat = [a for p in parts for a in p]
    return pl.pallas_call(
        functools.partial(_place_kernel, counts),
        in_specs=[pl.BlockSpec(memory_space=pltpu.SMEM)]
        + [pl.BlockSpec(memory_space=pltpu.VMEM) for _ in flat],
        out_specs=pl.BlockSpec(memory_space=pltpu.VMEM),
        out_shape=jax.ShapeDtypeStruct((sum(counts), PANEL, cut), jnp.bfloat16),
        compiler_params=pltpu.CompilerParams(vmem_limit_bytes=16 << 20),
        name="place",
    )(where, *flat)


def _total_kernel(low_ref, high_ref, o_ref):
    total = low_ref[0].astype(jnp.float32) + high_ref[0].astype(jnp.float32)
    o_ref[...] = total.T


def _total(parts):
    groups, width, cut = parts.shape
    return pl.pallas_call(
        _total_kernel,
        grid=(NX,),
        in_specs=[
            pl.BlockSpec((1, width, cut), lambda i: (i, 0, 0)),
            pl.BlockSpec((1, width, cut), lambda i: (i + NX, 0, 0)),
        ],
        out_specs=pl.BlockSpec((cut, width), lambda i: (i, 0)),
        out_shape=jax.ShapeDtypeStruct((NX * cut, width), jnp.float32),
        compiler_params=pltpu.CompilerParams(vmem_limit_bytes=16 << 20),
        name="total",
    )(parts, parts)


def body(candidates, queries, out_factor, in_factor, panel_order):
    cand_rows, layer_count, features = candidates.shape
    width = queries.shape[0]
    out_units = out_factor.shape[1]
    in_units = in_factor.shape[1]
    groups = lax.axis_size("group")
    scale = 1.0 / (features * layer_count * groups) ** 0.5
    grads = queries.astype(jnp.float32).reshape(width, layer_count, out_units, in_units)
    left = jnp.einsum("lab,qlbc->qlac", out_factor, grads, precision=lax.Precision.HIGHEST)
    precond = jnp.einsum("qlac,lcd->qlad", left, in_factor, precision=lax.Precision.HIGHEST)
    panel = precond.reshape(width, layer_count * features).astype(jnp.bfloat16)
    flat = candidates.reshape(cand_rows, layer_count * features)
    x_index = lax.rem(lax.axis_index("group"), NX).reshape(1)

    slots, parts = [], []

    def meet(arrivals):
        pieces = [a for a, _ in arrivals]
        pieces += [_move(a, flip_core=True) for a, _ in arrivals]
        for dc in (0, 1):
            slots.extend((dz, dy, dc) for _, (dz, dy) in arrivals)
        own, *others = _score(x_index, pieces, flat, scale)
        parts.append([own] + [_group_move(o, d + 1) for d, o in enumerate(others)])

    of = ob = panel
    pf = pb = _move(panel, flip_y=True)
    meet([(of, (0, 0)), (pf, (0, 1))])
    for s in range(1, NZ // 2):
        of, ob = _move(of, dz=1), _move(ob, dz=-1)
        pf, pb = _move(pf, dz=1), _move(pb, dz=-1)
        meet([(of, (-s, 0)), (ob, (s, 0)), (pf, (-s, 1)), (pb, (s, 1))])
    s = NZ // 2
    meet([(_move(of, dz=1), (-s, 0)), (_move(pb, dz=-1), (s, 1))])

    me = lax.axis_index("blk")
    z, rest = me // 4, me % 4
    dz = jnp.array([t[0] for t in slots], jnp.int32)
    flip = jnp.array([t[1] * 2 + t[2] for t in slots], jnp.int32)
    source = ((z + dz) % NZ) * 4 + (rest ^ flip)
    places = jnp.arange(panel_order.shape[0], dtype=jnp.int32)
    where = jnp.sum(jnp.where(panel_order[None, :] == source[:, None], places[None, :], 0), axis=1).astype(jnp.int32)
    buffer = _place(parts, where).reshape(groups, -1, cand_rows // NX)
    moved = lax.all_to_all(buffer, "group", split_axis=0, concat_axis=0, tiled=True)
    return _total(moved)


def solution(mesh):
    in_specs = (
        P("blk", "group", None),
        P("blk", "group", None),
        P("group", None, None),
        P("group", None, None),
        P(),
    )
    out_specs = P("blk", "group")
    return jax.shard_map(body, mesh=mesh, in_specs=in_specs, out_specs=out_specs, check_vma=False)
```

```python
import functools

import jax
import jax.numpy as jnp
from jax import lax
from jax.experimental import pallas as pl
from jax.experimental.pallas import tpu as pltpu
from jax.sharding import PartitionSpec as P

NZ = 8
PANEL = 32
CBLK = 256
SBLK = 512


def _route(x, target):
    return lax.ppermute(x, "blk", [(i, target(*divmod(i, 4))) for i in range(NZ * 4)])


def _along(x):
    return _route(x, lambda z, rest: ((z + (1 if rest % 2 == 0 else -1)) % NZ) * 4 + rest)


def _swap_core(x):
    return _route(x, lambda z, rest: z * 4 + (rest ^ 1))


def _swap_y(x):
    return _route(x, lambda z, rest: z * 4 + (rest ^ 2))


def _score_kernel(scale, count, *refs):
    c_ref, o_ref = refs[count], refs[count + 1]
    panels = jnp.concatenate([r[...] for r in refs[:count]], axis=0)
    part = lax.dot_general(
        panels, c_ref[...], (((1,), (1,)), ((), ())), preferred_element_type=jnp.float32
    )
    o_ref[...] = (part * scale).astype(o_ref.dtype)


def _score(pieces, flat, scale):
    rows, feats = flat.shape
    n = sum(p.shape[0] for p in pieces)
    return pl.pallas_call(
        functools.partial(_score_kernel, scale, len(pieces)),
        grid=(rows // SBLK,),
        in_specs=[pl.BlockSpec(p.shape, lambda i: (0, 0)) for p in pieces]
        + [pl.BlockSpec((SBLK, feats), lambda i: (i, 0))],
        out_specs=pl.BlockSpec((n, SBLK), lambda i: (0, i)),
        out_shape=jax.ShapeDtypeStruct((n, rows), jnp.bfloat16),
        compiler_params=pltpu.CompilerParams(vmem_limit_bytes=24 << 20),
        cost_estimate=pl.CostEstimate(
            flops=2 * n * rows * feats, bytes_accessed=2 * (rows * feats + n * feats + n * rows), transcendentals=0
        ),
        name="score",
    )(*pieces, flat)


def _place_kernel(counts, where_ref, *refs):
    out = refs[-1]
    slot = 0
    for ref, count in zip(refs[:-1], counts):
        for i in range(count):
            out[where_ref[slot]] = ref[i * PANEL : (i + 1) * PANEL, :]
            slot += 1


def _place(parts, where):
    counts = [p.shape[0] // PANEL for p in parts]
    rows = parts[0].shape[1]
    return pl.pallas_call(
        functools.partial(_place_kernel, counts),
        in_specs=[pl.BlockSpec(memory_space=pltpu.SMEM)]
        + [pl.BlockSpec(memory_space=pltpu.VMEM) for _ in parts],
        out_specs=pl.BlockSpec(memory_space=pltpu.VMEM),
        out_shape=jax.ShapeDtypeStruct((sum(counts), PANEL, rows), jnp.bfloat16),
        compiler_params=pltpu.CompilerParams(vmem_limit_bytes=12 << 20),
        name="place",
    )(where, *parts)


def _total_kernel(in_ref, o_ref):
    total = in_ref[0].astype(jnp.float32)
    for g in range(1, in_ref.shape[0]):
        total += in_ref[g].astype(jnp.float32)
    o_ref[...] = total.T


def _total(parts):
    groups, width, rows = parts.shape
    return pl.pallas_call(
        _total_kernel,
        grid=(rows // CBLK,),
        in_specs=[pl.BlockSpec((groups, width, CBLK), lambda i: (0, 0, i))],
        out_specs=pl.BlockSpec((CBLK, width), lambda i: (i, 0)),
        out_shape=jax.ShapeDtypeStruct((rows, width), jnp.float32),
        compiler_params=pltpu.CompilerParams(vmem_limit_bytes=12 << 20),
        name="total",
    )(parts)


def body(candidates, queries, out_factor, in_factor, panel_order):
    cand_rows, layer_count, features = candidates.shape
    width = queries.shape[0]
    out_units = out_factor.shape[1]
    in_units = in_factor.shape[1]
    groups = lax.axis_size("group")
    scale = 1.0 / (features * layer_count * groups) ** 0.5
    grads = queries.astype(jnp.float32).reshape(width, layer_count, out_units, in_units)
    left = jnp.einsum("lab,qlbc->qlac", out_factor, grads, precision=lax.Precision.HIGHEST)
    precond = jnp.einsum("qlac,lcd->qlad", left, in_factor, precision=lax.Precision.HIGHEST)
    panel = precond.reshape(width, layer_count * features).astype(jnp.bfloat16)
    flat = candidates.reshape(cand_rows, layer_count * features)

    flat = pltpu.with_memory_space_constraint(flat, pltpu.HBM)
    me = lax.axis_index("blk")
    z, rest = me // 4, me % 4
    core = me % 2
    up = 1 - 2 * core

    sources = []

    def note(dz, dy):
        sources.append(((z + dz) % NZ) * 4 + (rest ^ (2 * dy)))
        sources.append(((z + dz) % NZ) * 4 + (rest ^ (2 * dy) ^ 1))

    def note_far(dz, dy):
        sources.append(((z + dz) % NZ) * 4 + (rest ^ (2 * dy) ^ 1))
        sources.append(((z + dz) % NZ) * 4 + (rest ^ (2 * dy)))

    across = _swap_y(panel)
    near = jnp.concatenate([panel, _swap_core(panel)], axis=0)
    far = jnp.concatenate([across, _swap_core(across)], axis=0)
    note(0, 0)
    note(0, 1)
    steps = [_score([near, far], flat, scale)]
    for s in range(1, NZ // 2):
        near, far = _along(near), _along(far)
        steps[-1], near = lax.optimization_barrier((steps[-1], near))
        steps[-1], far = lax.optimization_barrier((steps[-1], far))
        note(-s * up, 0)
        note_far(s * up, 0)
        note(-s * up, 1)
        note_far(s * up, 1)
        steps.append(_score([near, _swap_core(near), far, _swap_core(far)], flat, scale))
    last = _along(jnp.where(core == 0, near, far))
    steps[-1], last = lax.optimization_barrier((steps[-1], last))
    note(NZ // 2, core)
    note_far(NZ // 2, 1 - core)
    steps.append(_score([last, _swap_core(last)], flat, scale))

    source = jnp.stack(sources)
    places = jnp.arange(panel_order.shape[0], dtype=jnp.int32)
    where = jnp.sum(jnp.where(panel_order[None, :] == source[:, None], places[None, :], 0), axis=1).astype(jnp.int32)
    buffer = _place(steps, where).reshape(groups, -1, cand_rows)
    parts = lax.all_to_all(buffer, "group", split_axis=0, concat_axis=0, tiled=True)
    return _total(parts)


def solution(mesh):
    in_specs = (
        P("blk", "group", None),
        P("blk", "group", None),
        P("group", None, None),
        P("group", None, None),
        P(),
    )
    out_specs = P("blk", "group")
    return jax.shard_map(body, mesh=mesh, in_specs=in_specs, out_specs=out_specs, check_vma=False)
```

```python
import functools

import jax
import jax.numpy as jnp
from jax import lax
from jax.experimental import pallas as pl
from jax.experimental.pallas import tpu as pltpu
from jax.sharding import PartitionSpec as P

NZ = 8
PANEL = 32
CBLK = 256


def _route(x, target):
    return lax.ppermute(x, "blk", [(i, target(*divmod(i, 4))) for i in range(NZ * 4)])


def _along(x):
    return _route(x, lambda z, rest: ((z + (1 if rest % 2 == 0 else -1)) % NZ) * 4 + rest)


def _swap_core(x):
    return _route(x, lambda z, rest: z * 4 + (rest ^ 1))


def _swap_y(x):
    return _route(x, lambda z, rest: z * 4 + (rest ^ 2))


def _joined_kernel(*refs):
    *parts, out = refs
    at = 0
    for r in parts:
        out[at : at + PANEL, :] = r[:PANEL, :]
        at += PANEL


def _joined(*parts):
    feats = parts[0].shape[1]
    return pl.pallas_call(
        _joined_kernel,
        in_specs=[pl.BlockSpec(memory_space=pltpu.VMEM) for _ in parts],
        out_specs=pl.BlockSpec(memory_space=pltpu.VMEM),
        out_shape=jax.ShapeDtypeStruct((len(parts) * PANEL, feats), parts[0].dtype),
        compiler_params=pltpu.CompilerParams(vmem_limit_bytes=4 << 20),
        name="joined",
    )(*parts)


def _score_kernel(scale, count, *refs):
    c_ref, o_ref = refs[count], refs[count + 1]
    panels = jnp.concatenate([r[...] for r in refs[:count]], axis=0)
    for i in range(c_ref.shape[0] // CBLK):
        block = slice(i * CBLK, (i + 1) * CBLK)
        part = lax.dot_general(
            panels, c_ref[block, :], (((1,), (1,)), ((), ())), preferred_element_type=jnp.float32
        )
        o_ref[:, block] = (part * scale).astype(o_ref.dtype)


def _score(pieces, flat, scale):
    rows, feats = flat.shape
    n = sum(p.shape[0] for p in pieces)
    return pl.pallas_call(
        functools.partial(_score_kernel, scale, len(pieces)),
        in_specs=[pl.BlockSpec(memory_space=pltpu.VMEM) for _ in range(len(pieces) + 1)],
        out_specs=pl.BlockSpec(memory_space=pltpu.VMEM),
        out_shape=jax.ShapeDtypeStruct((n, rows), jnp.bfloat16),
        compiler_params=pltpu.CompilerParams(vmem_limit_bytes=16 << 20),
        cost_estimate=pl.CostEstimate(
            flops=2 * n * rows * feats, bytes_accessed=2 * (rows * feats + n * feats + n * rows), transcendentals=0
        ),
        name="score",
    )(*pieces, flat)


def _place_kernel(counts, where_ref, *refs):
    out = refs[-1]
    slot = 0
    for ref, count in zip(refs[:-1], counts):
        for i in range(count):
            out[where_ref[slot]] = ref[i * PANEL : (i + 1) * PANEL, :]
            slot += 1


def _place(parts, where):
    counts = [p.shape[0] // PANEL for p in parts]
    rows = parts[0].shape[1]
    return pl.pallas_call(
        functools.partial(_place_kernel, counts),
        in_specs=[pl.BlockSpec(memory_space=pltpu.SMEM)]
        + [pl.BlockSpec(memory_space=pltpu.VMEM) for _ in parts],
        out_specs=pl.BlockSpec(memory_space=pltpu.VMEM),
        out_shape=jax.ShapeDtypeStruct((sum(counts), PANEL, rows), jnp.bfloat16),
        compiler_params=pltpu.CompilerParams(vmem_limit_bytes=12 << 20),
        name="place",
    )(where, *parts)


def _total_kernel(in_ref, o_ref):
    total = in_ref[0].astype(jnp.float32)
    for g in range(1, in_ref.shape[0]):
        total += in_ref[g].astype(jnp.float32)
    o_ref[...] = total.T


def _total(parts):
    groups, width, rows = parts.shape
    return pl.pallas_call(
        _total_kernel,
        grid=(rows // CBLK,),
        in_specs=[pl.BlockSpec((groups, width, CBLK), lambda i: (0, 0, i))],
        out_specs=pl.BlockSpec((CBLK, width), lambda i: (i, 0)),
        out_shape=jax.ShapeDtypeStruct((rows, width), jnp.float32),
        compiler_params=pltpu.CompilerParams(vmem_limit_bytes=12 << 20),
        name="total",
    )(parts)


def body(candidates, queries, out_factor, in_factor, panel_order):
    cand_rows, layer_count, features = candidates.shape
    width = queries.shape[0]
    out_units = out_factor.shape[1]
    in_units = in_factor.shape[1]
    groups = lax.axis_size("group")
    scale = 1.0 / (features * layer_count * groups) ** 0.5
    grads = queries.astype(jnp.float32).reshape(width, layer_count, out_units, in_units)
    left = jnp.einsum("lab,qlbc->qlac", out_factor, grads, precision=lax.Precision.HIGHEST)
    precond = jnp.einsum("qlac,lcd->qlad", left, in_factor, precision=lax.Precision.HIGHEST)
    panel = precond.reshape(width, layer_count * features).astype(jnp.bfloat16)
    flat = candidates.reshape(cand_rows, layer_count * features)

    flat = pltpu.with_memory_space_constraint(flat, pltpu.VMEM)
    me = lax.axis_index("blk")
    z, rest = me // 4, me % 4
    core = me % 2
    up = 1 - 2 * core

    sources = []

    def note(dz, dy):
        sources.append(((z + dz) % NZ) * 4 + (rest ^ (2 * dy)))
        sources.append(((z + dz) % NZ) * 4 + (rest ^ (2 * dy) ^ 1))

    def note_far(dz, dy):
        sources.append(((z + dz) % NZ) * 4 + (rest ^ (2 * dy) ^ 1))
        sources.append(((z + dz) % NZ) * 4 + (rest ^ (2 * dy)))

    note(0, 0)
    note(0, 1)
    for s in range(1, NZ // 2):
        note(-s * up, 0)
        note_far(s * up, 0)
        note(-s * up, 1)
        note_far(s * up, 1)
    for dy in (0, 1):
        sources.append(((z + NZ // 2) % NZ) * 4 + (rest ^ (2 * dy)))
        sources.append(((z + NZ // 2) % NZ) * 4 + (rest ^ (2 * dy) ^ 1))
    source = jnp.stack(sources)
    places = jnp.arange(panel_order.shape[0], dtype=jnp.int32)
    where = jnp.sum(jnp.where(panel_order[None, :] == source[:, None], places[None, :], 0), axis=1).astype(jnp.int32)

    steps = []

    def after(step, x):
        steps[step], x = lax.optimization_barrier((steps[step], x))
        return x

    across = _swap_y(panel)
    near = _joined(panel, _swap_core(panel))
    steps.append(_score([near], flat, scale))
    steps[0], where, across = lax.optimization_barrier((steps[0], where, across))
    far = _joined(across, _swap_core(across))
    steps.append(_score([far], flat, scale))
    for s in range(1, NZ // 2):
        near, far = _along(near), _along(far)
        far = after(s, far)
        steps.append(_score([near, _swap_core(near), far, _swap_core(far)], flat, scale))
    near, far = _along(_joined(near)), _along(_joined(far))
    far = after(NZ // 2, far)
    steps.append(_score([near, _swap_core(near), far, _swap_core(far)], flat, scale))
    buffer = _place(steps, where).reshape(groups, -1, cand_rows)
    parts = lax.all_to_all(buffer, "group", split_axis=0, concat_axis=0, tiled=True)
    return _total(parts)


def solution(mesh):
    in_specs = (
        P("blk", "group", None),
        P("blk", "group", None),
        P("group", None, None),
        P("group", None, None),
        P(),
    )
    out_specs = P("blk", "group")
    return jax.shard_map(body, mesh=mesh, in_specs=in_specs, out_specs=out_specs, check_vma=False)
```

```python
import functools

import jax
import jax.numpy as jnp
from jax import lax
from jax.experimental import pallas as pl
from jax.experimental.pallas import tpu as pltpu
from jax.sharding import PartitionSpec as P

NZ = 8
PANEL = 32
LANES = 128
CBLK = 256


def _route(x, target):
    return lax.ppermute(x, "blk", [(i, target(*divmod(i, 4))) for i in range(NZ * 4)])


def _along(x):
    return _route(x, lambda z, rest: ((z + (1 if rest % 2 == 0 else -1)) % NZ) * 4 + rest)


def _across(x):
    return _route(x, lambda z, rest: ((z + (1 if rest % 2 == 0 else -1)) % NZ) * 4 + (rest ^ 2))


def _swap_core(x):
    return _route(x, lambda z, rest: z * 4 + (rest ^ 1))


def _swap_y(x):
    return _route(x, lambda z, rest: z * 4 + (rest ^ 2))


def _precond_kernel(a_ref, b_ref, q_ref, o_ref, one_ref, two_ref, left_ref):
    width = q_ref.shape[0]
    tiles = q_ref.shape[1] // LANES
    half = LANES // 2
    zero = jnp.zeros((half, half), jnp.float32)
    b = b_ref[...]
    right = jnp.concatenate(
        [
            jnp.concatenate([b, zero, zero, b], axis=1),
            jnp.concatenate([zero, b, b, zero], axis=1),
        ],
        axis=0,
    )
    rows = jnp.concatenate([q_ref[:, t * LANES : (t + 1) * LANES] for t in range(tiles)], axis=0)
    done = None
    for _ in range(3):
        term = right.astype(jnp.bfloat16)
        right = right - term.astype(jnp.float32)
        part = jnp.dot(rows, term, preferred_element_type=jnp.float32)
        done = part if done is None else done + part
    one_ref[...] = done[:, :LANES]
    two_ref[...] = done[:, LANES:]
    row = lax.broadcasted_iota(jnp.int32, (half, half), 0)
    col = lax.broadcasted_iota(jnp.int32, (half, half), 1)
    unit = jnp.where(col < half // 2, 2 * col, 2 * (col - half // 2) + 1)
    pick = jnp.where(row == unit, 1.0, 0.0).astype(jnp.float32)
    left_ref[...] = jnp.dot(
        a_ref[...], pick, precision=lax.Precision.HIGHEST, preferred_element_type=jnp.float32
    )
    even = left_ref[pl.ds(0, half // 2, stride=2), :]
    odd = left_ref[pl.ds(1, half // 2, stride=2), :]
    odd = jnp.concatenate([odd[:, half // 2 :], odd[:, : half // 2]], axis=1)
    left = jnp.concatenate([even, odd], axis=0)
    lanes = lax.broadcasted_iota(jnp.int32, (tiles, LANES), 1)
    chunk = 8
    for q0 in range(0, width, chunk):
        columns = [
            jnp.concatenate(
                [one_ref[pl.ds(q, tiles, stride=width), :], two_ref[pl.ds(q, tiles, stride=width), :]], axis=0
            )
            for q in range(q0, q0 + chunk)
        ]
        both = jnp.dot(
            left,
            jnp.concatenate(columns, axis=1),
            precision=lax.Precision.HIGHEST,
            preferred_element_type=jnp.float32,
        )
        for i in range(chunk):
            block = both[:, i * LANES : (i + 1) * LANES]
            one_ref[pl.ds(q0 + i, tiles, stride=width), :] = jnp.where(lanes < half, block[:tiles], block[tiles:])
    for t in range(tiles):
        o_ref[:, t * LANES : (t + 1) * LANES] = one_ref[t * width : (t + 1) * width, :].astype(o_ref.dtype)


def _precond(out_factor, in_factor, queries):
    width, feats = queries.shape
    rows = width * feats // LANES
    return pl.pallas_call(
        _precond_kernel,
        in_specs=[pl.BlockSpec(memory_space=pltpu.VMEM) for _ in range(3)],
        out_specs=pl.BlockSpec(memory_space=pltpu.VMEM),
        out_shape=jax.ShapeDtypeStruct((width, feats), jnp.bfloat16),
        scratch_shapes=[
            pltpu.VMEM((rows, LANES), jnp.float32),
            pltpu.VMEM((rows, LANES), jnp.float32),
            pltpu.VMEM(out_factor.shape, jnp.float32),
        ],
        compiler_params=pltpu.CompilerParams(vmem_limit_bytes=12 << 20),
        name="precond",
    )(out_factor, in_factor, queries)


def _joined_kernel(*refs):
    *parts, out = refs
    at = 0
    for r in parts:
        out[at : at + PANEL, :] = r[:PANEL, :]
        at += PANEL


def _joined(*parts):
    feats = parts[0].shape[1]
    return pl.pallas_call(
        _joined_kernel,
        in_specs=[pl.BlockSpec(memory_space=pltpu.VMEM) for _ in parts],
        out_specs=pl.BlockSpec(memory_space=pltpu.VMEM),
        out_shape=jax.ShapeDtypeStruct((len(parts) * PANEL, feats), parts[0].dtype),
        compiler_params=pltpu.CompilerParams(vmem_limit_bytes=4 << 20),
        name="joined",
    )(*parts)


def _score_kernel(scale, count, *refs):
    c_ref, o_ref = refs[count], refs[count + 1]
    panels = jnp.concatenate([r[...] for r in refs[:count]], axis=0)
    for i in range(c_ref.shape[0] // CBLK):
        block = slice(i * CBLK, (i + 1) * CBLK)
        part = lax.dot_general(
            panels, c_ref[block, :], (((1,), (1,)), ((), ())), preferred_element_type=jnp.float32
        )
        o_ref[:, block] = (part * scale).astype(o_ref.dtype)


def _score(pieces, flat, scale):
    rows, feats = flat.shape
    n = sum(p.shape[0] for p in pieces)
    return pl.pallas_call(
        functools.partial(_score_kernel, scale, len(pieces)),
        in_specs=[pl.BlockSpec(memory_space=pltpu.VMEM) for _ in range(len(pieces) + 1)],
        out_specs=pl.BlockSpec(memory_space=pltpu.VMEM),
        out_shape=jax.ShapeDtypeStruct((n, rows), jnp.bfloat16),
        compiler_params=pltpu.CompilerParams(vmem_limit_bytes=16 << 20),
        cost_estimate=pl.CostEstimate(
            flops=2 * n * rows * feats, bytes_accessed=2 * (rows * feats + n * feats + n * rows), transcendentals=0
        ),
        name="score",
    )(*pieces, flat)


def _place_kernel(counts, where_ref, *refs):
    out = refs[-1]
    slot = 0
    for ref, count in zip(refs[:-1], counts):
        for i in range(count):
            out[where_ref[slot]] = ref[i * PANEL : (i + 1) * PANEL, :]
            slot += 1


def _place(parts, where):
    counts = [p.shape[0] // PANEL for p in parts]
    rows = parts[0].shape[1]
    return pl.pallas_call(
        functools.partial(_place_kernel, counts),
        in_specs=[pl.BlockSpec(memory_space=pltpu.SMEM)]
        + [pl.BlockSpec(memory_space=pltpu.VMEM) for _ in parts],
        out_specs=pl.BlockSpec(memory_space=pltpu.VMEM),
        out_shape=jax.ShapeDtypeStruct((sum(counts), PANEL, rows), jnp.bfloat16),
        compiler_params=pltpu.CompilerParams(vmem_limit_bytes=12 << 20),
        name="place",
    )(where, *parts)


def _total_kernel(in_ref, o_ref):
    total = in_ref[0].astype(jnp.float32)
    for g in range(1, in_ref.shape[0]):
        total += in_ref[g].astype(jnp.float32)
    o_ref[...] = total.T


def _total(parts):
    groups, width, rows = parts.shape
    return pl.pallas_call(
        _total_kernel,
        grid=(rows // CBLK,),
        in_specs=[pl.BlockSpec((groups, width, CBLK), lambda i: (0, 0, i))],
        out_specs=pl.BlockSpec((CBLK, width), lambda i: (i, 0)),
        out_shape=jax.ShapeDtypeStruct((rows, width), jnp.float32),
        compiler_params=pltpu.CompilerParams(vmem_limit_bytes=12 << 20),
        name="total",
    )(parts)


def body(candidates, queries, out_factor, in_factor, panel_order):
    cand_rows, layer_count, features = candidates.shape
    width = queries.shape[0]
    groups = lax.axis_size("group")
    scale = 1.0 / (features * layer_count * groups) ** 0.5
    panel = _precond(out_factor[0], in_factor[0], queries.reshape(width, layer_count * features))
    flat = candidates.reshape(cand_rows, layer_count * features)

    flat = pltpu.with_memory_space_constraint(flat, pltpu.VMEM)
    me = lax.axis_index("blk")
    z, rest = me // 4, me % 4
    core = me % 2
    up = 1 - 2 * core

    sources = []

    def note(dz, dy):
        sources.append(((z + dz) % NZ) * 4 + (rest ^ (2 * dy)))
        sources.append(((z + dz) % NZ) * 4 + (rest ^ (2 * dy) ^ 1))

    def note_far(dz, dy):
        sources.append(((z + dz) % NZ) * 4 + (rest ^ (2 * dy) ^ 1))
        sources.append(((z + dz) % NZ) * 4 + (rest ^ (2 * dy)))

    note(0, 0)
    for s in range(1, NZ // 2):
        note(-s * up, 0)
        note_far(s * up, 0)
        note(-s * up, 1)
        note_far(s * up, 1)
        if s == 2:
            note(0, 1)
    for dy in (0, 1):
        sources.append(((z + NZ // 2) % NZ) * 4 + (rest ^ (2 * dy)))
        sources.append(((z + NZ // 2) % NZ) * 4 + (rest ^ (2 * dy) ^ 1))
    source = jnp.stack(sources)
    places = jnp.arange(panel_order.shape[0], dtype=jnp.int32)
    where = jnp.sum(jnp.where(panel_order[None, :] == source[:, None], places[None, :], 0), axis=1).astype(jnp.int32)

    steps = []

    near = _joined(panel, _swap_core(panel))
    near, where = lax.optimization_barrier((near, where))
    pieces = [near]
    start = near
    near, far = _along(start), _across(start)
    more = []
    for s in range(1, NZ // 2 + 1):
        if s == NZ // 2 - 1:
            cut = _joined(near)
            near, cut, pieces[0] = lax.optimization_barrier((near, cut, pieces[0]))
        else:
            near, pieces[0] = lax.optimization_barrier((near, pieces[0]))
        steps.append(_score(pieces, flat, scale))
        if s == 1:
            steps[0], far, start = lax.optimization_barrier((steps[0], far, start))
            more = [_swap_y(start)]
        else:
            steps[-1], far = lax.optimization_barrier((steps[-1], far))
        pieces = [near, _swap_core(near), far, _swap_core(far)]
        if s == 2:
            pieces += more
        if s < NZ // 2 - 1:
            near, far = _along(near), _along(far)
        elif s == NZ // 2 - 1:
            near, far = _along(cut), _along(_joined(far))
    steps.append(_score(pieces, flat, scale))
    buffer = _place(steps, where).reshape(groups, -1, cand_rows)
    parts = lax.all_to_all(buffer, "group", split_axis=0, concat_axis=0, tiled=True)
    return _total(parts)


def solution(mesh):
    in_specs = (
        P("blk", "group", None),
        P("blk", "group", None),
        P("group", None, None),
        P("group", None, None),
        P(),
    )
    out_specs = P("blk", "group")
    return jax.shard_map(body, mesh=mesh, in_specs=in_specs, out_specs=out_specs, check_vma=False)
```

```python
import functools

import jax
import jax.numpy as jnp
from jax import lax
from jax.experimental import pallas as pl
from jax.experimental.pallas import tpu as pltpu
from jax.sharding import PartitionSpec as P

NZ = 8
PANEL = 32
LANES = 128
CBLK = 256


def _route(x, target):
    return lax.ppermute(x, "blk", [(i, target(*divmod(i, 4))) for i in range(NZ * 4)])


def _along(x):
    return _route(x, lambda z, rest: ((z + (1 if rest % 2 == 0 else -1)) % NZ) * 4 + rest)


def _swap_core(x):
    return _route(x, lambda z, rest: z * 4 + (rest ^ 1))


def _swap_y(x):
    return _route(x, lambda z, rest: z * 4 + (rest ^ 2))


def _precond_kernel(a_ref, b_ref, q_ref, o_ref, one_ref, two_ref, left_ref):
    width = q_ref.shape[0]
    tiles = q_ref.shape[1] // LANES
    half = LANES // 2
    zero = jnp.zeros((half, half), jnp.float32)
    b = b_ref[...]
    right = jnp.concatenate(
        [
            jnp.concatenate([b, zero, zero, b], axis=1),
            jnp.concatenate([zero, b, b, zero], axis=1),
        ],
        axis=0,
    )
    rows = jnp.concatenate([q_ref[:, t * LANES : (t + 1) * LANES] for t in range(tiles)], axis=0)
    done = None
    for _ in range(3):
        term = right.astype(jnp.bfloat16)
        right = right - term.astype(jnp.float32)
        part = jnp.dot(rows, term, preferred_element_type=jnp.float32)
        done = part if done is None else done + part
    one_ref[...] = done[:, :LANES]
    two_ref[...] = done[:, LANES:]
    row = lax.broadcasted_iota(jnp.int32, (half, half), 0)
    col = lax.broadcasted_iota(jnp.int32, (half, half), 1)
    unit = jnp.where(col < half // 2, 2 * col, 2 * (col - half // 2) + 1)
    pick = jnp.where(row == unit, 1.0, 0.0).astype(jnp.float32)
    left_ref[...] = jnp.dot(
        a_ref[...], pick, precision=lax.Precision.HIGHEST, preferred_element_type=jnp.float32
    )
    even = left_ref[pl.ds(0, half // 2, stride=2), :]
    odd = left_ref[pl.ds(1, half // 2, stride=2), :]
    odd = jnp.concatenate([odd[:, half // 2 :], odd[:, : half // 2]], axis=1)
    left = jnp.concatenate([even, odd], axis=0)
    lanes = lax.broadcasted_iota(jnp.int32, (tiles, LANES), 1)
    chunk = 8
    for q0 in range(0, width, chunk):
        columns = [
            jnp.concatenate(
                [one_ref[pl.ds(q, tiles, stride=width), :], two_ref[pl.ds(q, tiles, stride=width), :]], axis=0
            )
            for q in range(q0, q0 + chunk)
        ]
        both = jnp.dot(
            left,
            jnp.concatenate(columns, axis=1),
            precision=lax.Precision.HIGHEST,
            preferred_element_type=jnp.float32,
        )
        for i in range(chunk):
            block = both[:, i * LANES : (i + 1) * LANES]
            one_ref[pl.ds(q0 + i, tiles, stride=width), :] = jnp.where(lanes < half, block[:tiles], block[tiles:])
    for t in range(tiles):
        o_ref[:, t * LANES : (t + 1) * LANES] = one_ref[t * width : (t + 1) * width, :].astype(o_ref.dtype)


def _precond(out_factor, in_factor, queries):
    width, feats = queries.shape
    rows = width * feats // LANES
    return pl.pallas_call(
        _precond_kernel,
        in_specs=[pl.BlockSpec(memory_space=pltpu.VMEM) for _ in range(3)],
        out_specs=pl.BlockSpec(memory_space=pltpu.VMEM),
        out_shape=jax.ShapeDtypeStruct((width, feats), jnp.bfloat16),
        scratch_shapes=[
            pltpu.VMEM((rows, LANES), jnp.float32),
            pltpu.VMEM((rows, LANES), jnp.float32),
            pltpu.VMEM(out_factor.shape, jnp.float32),
        ],
        compiler_params=pltpu.CompilerParams(vmem_limit_bytes=12 << 20),
        name="precond",
    )(*(pltpu.with_memory_space_constraint(x, pltpu.HBM) for x in (out_factor, in_factor, queries)))


def _joined_kernel(*refs):
    *parts, out = refs
    at = 0
    for r in parts:
        out[at : at + PANEL, :] = r[:PANEL, :]
        at += PANEL


def _joined(*parts):
    feats = parts[0].shape[1]
    return pl.pallas_call(
        _joined_kernel,
        in_specs=[pl.BlockSpec(memory_space=pltpu.VMEM) for _ in parts],
        out_specs=pl.BlockSpec(memory_space=pltpu.VMEM),
        out_shape=jax.ShapeDtypeStruct((len(parts) * PANEL, feats), parts[0].dtype),
        compiler_params=pltpu.CompilerParams(vmem_limit_bytes=4 << 20),
        name="joined",
    )(*parts)


def _score_kernel(scale, count, *refs):
    c_ref, o_ref = refs[count], refs[count + 1]
    panels = jnp.concatenate([r[...] for r in refs[:count]], axis=0)
    for i in range(c_ref.shape[0] // CBLK):
        block = slice(i * CBLK, (i + 1) * CBLK)
        part = lax.dot_general(
            panels, c_ref[block, :], (((1,), (1,)), ((), ())), preferred_element_type=jnp.float32
        )
        o_ref[:, block] = (part * scale).astype(o_ref.dtype)


def _score(pieces, flat, scale):
    rows, feats = flat.shape
    n = sum(p.shape[0] for p in pieces)
    return pl.pallas_call(
        functools.partial(_score_kernel, scale, len(pieces)),
        in_specs=[pl.BlockSpec(memory_space=pltpu.VMEM) for _ in range(len(pieces) + 1)],
        out_specs=pl.BlockSpec(memory_space=pltpu.VMEM),
        out_shape=jax.ShapeDtypeStruct((n, rows), jnp.bfloat16),
        compiler_params=pltpu.CompilerParams(vmem_limit_bytes=16 << 20),
        cost_estimate=pl.CostEstimate(
            flops=2 * n * rows * feats, bytes_accessed=2 * (rows * feats + n * feats + n * rows), transcendentals=0
        ),
        name="score",
    )(*pieces, flat)


def _place_kernel(counts, where_ref, *refs):
    out = refs[-1]
    slot = 0
    for ref, count in zip(refs[:-1], counts):
        for i in range(count):
            out[where_ref[slot]] = ref[i * PANEL : (i + 1) * PANEL, :]
            slot += 1


def _place(parts, where):
    counts = [p.shape[0] // PANEL for p in parts]
    rows = parts[0].shape[1]
    return pl.pallas_call(
        functools.partial(_place_kernel, counts),
        in_specs=[pl.BlockSpec(memory_space=pltpu.SMEM)]
        + [pl.BlockSpec(memory_space=pltpu.VMEM) for _ in parts],
        out_specs=pl.BlockSpec(memory_space=pltpu.VMEM),
        out_shape=jax.ShapeDtypeStruct((sum(counts), PANEL, rows), jnp.bfloat16),
        compiler_params=pltpu.CompilerParams(vmem_limit_bytes=12 << 20),
        name="place",
    )(where, *parts)


def _total_kernel(in_ref, o_ref):
    total = in_ref[0].astype(jnp.float32)
    for g in range(1, in_ref.shape[0]):
        total += in_ref[g].astype(jnp.float32)
    o_ref[...] = total.T


def _total(parts):
    groups, width, rows = parts.shape
    return pl.pallas_call(
        _total_kernel,
        grid=(rows // CBLK,),
        in_specs=[pl.BlockSpec((groups, width, CBLK), lambda i: (0, 0, i))],
        out_specs=pl.BlockSpec((CBLK, width), lambda i: (i, 0)),
        out_shape=jax.ShapeDtypeStruct((rows, width), jnp.float32),
        compiler_params=pltpu.CompilerParams(vmem_limit_bytes=12 << 20),
        name="total",
    )(parts)


def body(candidates, queries, out_factor, in_factor, panel_order):
    cand_rows, layer_count, features = candidates.shape
    width = queries.shape[0]
    groups = lax.axis_size("group")
    scale = 1.0 / (features * layer_count * groups) ** 0.5
    panel = _precond(out_factor[0], in_factor[0], queries.reshape(width, layer_count * features))
    flat = candidates.reshape(cand_rows, layer_count * features)

    flat = pltpu.with_memory_space_constraint(flat, pltpu.VMEM)
    me = lax.axis_index("blk")
    z, rest = me // 4, me % 4
    core = me % 2
    up = 1 - 2 * core

    sources = []

    def note(dz, dy):
        sources.append(((z + dz) % NZ) * 4 + (rest ^ (2 * dy)))
        sources.append(((z + dz) % NZ) * 4 + (rest ^ (2 * dy) ^ 1))

    def note_far(dz, dy):
        sources.append(((z + dz) % NZ) * 4 + (rest ^ (2 * dy) ^ 1))
        sources.append(((z + dz) % NZ) * 4 + (rest ^ (2 * dy)))

    note(0, 0)
    note(0, 1)
    for s in range(1, NZ // 2):
        note(-s * up, 0)
        note_far(s * up, 0)
        note(-s * up, 1)
        note_far(s * up, 1)
    for dy in (0, 1):
        sources.append(((z + NZ // 2) % NZ) * 4 + (rest ^ (2 * dy)))
        sources.append(((z + NZ // 2) % NZ) * 4 + (rest ^ (2 * dy) ^ 1))
    source = jnp.stack(sources)
    places = jnp.arange(panel_order.shape[0], dtype=jnp.int32)
    where = jnp.sum(jnp.where(panel_order[None, :] == source[:, None], places[None, :], 0), axis=1).astype(jnp.int32)

    steps = []

    across = _swap_y(panel)
    near = _joined(panel, _swap_core(panel))
    near, where = lax.optimization_barrier((near, where))
    start = near
    near = _along(near)
    near, across = lax.optimization_barrier((near, across))
    home = _joined(across, _swap_core(across))
    far = _along(home)
    pieces = [start, home]
    for s in range(1, NZ // 2):
        if s == NZ // 2 - 1:
            cut = _joined(near)
            near, cut, pieces[0] = lax.optimization_barrier((near, cut, pieces[0]))
        elif s > 1:
            near, pieces[0] = lax.optimization_barrier((near, pieces[0]))
        steps.append(_score(pieces, flat, scale))
        if s == NZ // 2 - 1:
            steps[-1], last = lax.optimization_barrier((steps[-1], _along(cut)))
            last, far = lax.optimization_barrier((last, far))
        steps[-1], far = lax.optimization_barrier((steps[-1], far))
        pieces = [near, _swap_core(near), far, _swap_core(far)]
        if s < NZ // 2 - 1:
            near, far = _along(near), _along(far)
    beyond = _swap_y(last)
    steps.append(_score(pieces, flat, scale))
    steps[-1], beyond = lax.optimization_barrier((steps[-1], beyond))
    steps.append(_score([last, _swap_core(last), beyond, _swap_core(beyond)], flat, scale))
    buffer = _place(steps, where).reshape(groups, -1, cand_rows)
    parts = lax.all_to_all(buffer, "group", split_axis=0, concat_axis=0, tiled=True)
    return _total(parts)


def solution(mesh):
    in_specs = (
        P("blk", "group", None),
        P("blk", "group", None),
        P("group", None, None),
        P("group", None, None),
        P(),
    )
    out_specs = P("blk", "group")
    return jax.shard_map(body, mesh=mesh, in_specs=in_specs, out_specs=out_specs, check_vma=False)
```

```python
import functools

import jax
import jax.numpy as jnp
from jax import lax
from jax.experimental import pallas as pl
from jax.experimental.pallas import tpu as pltpu
from jax.sharding import PartitionSpec as P

NZ = 8
PANEL = 32
LANES = 128
CBLK = 256


def _route(x, target):
    return lax.ppermute(x, "blk", [(i, target(*divmod(i, 4))) for i in range(NZ * 4)])


def _along(x):
    return _route(x, lambda z, rest: ((z + (1 if rest % 2 == 0 else -1)) % NZ) * 4 + rest)


def _swap_core(x):
    return _route(x, lambda z, rest: z * 4 + (rest ^ 1))


def _swap_y(x):
    return _route(x, lambda z, rest: z * 4 + (rest ^ 2))


def _precond_kernel(a_ref, b_ref, q_ref, o_ref, one_ref, two_ref, left_ref):
    width = q_ref.shape[0]
    tiles = q_ref.shape[1] // LANES
    half = LANES // 2
    zero = jnp.zeros((half, half), jnp.float32)
    b = b_ref[...]
    right = jnp.concatenate(
        [
            jnp.concatenate([b, zero, zero, b], axis=1),
            jnp.concatenate([zero, b, b, zero], axis=1),
        ],
        axis=0,
    )
    rows = jnp.concatenate([q_ref[:, t * LANES : (t + 1) * LANES] for t in range(tiles)], axis=0)
    done = None
    for _ in range(3):
        term = right.astype(jnp.bfloat16)
        right = right - term.astype(jnp.float32)
        part = jnp.dot(rows, term, preferred_element_type=jnp.float32)
        done = part if done is None else done + part
    one_ref[...] = done[:, :LANES]
    two_ref[...] = done[:, LANES:]
    row = lax.broadcasted_iota(jnp.int32, (half, half), 0)
    col = lax.broadcasted_iota(jnp.int32, (half, half), 1)
    unit = jnp.where(col < half // 2, 2 * col, 2 * (col - half // 2) + 1)
    pick = jnp.where(row == unit, 1.0, 0.0).astype(jnp.float32)
    left_ref[...] = jnp.dot(
        a_ref[...], pick, precision=lax.Precision.HIGHEST, preferred_element_type=jnp.float32
    )
    even = left_ref[pl.ds(0, half // 2, stride=2), :]
    odd = left_ref[pl.ds(1, half // 2, stride=2), :]
    odd = jnp.concatenate([odd[:, half // 2 :], odd[:, : half // 2]], axis=1)
    left = jnp.concatenate([even, odd], axis=0)
    lanes = lax.broadcasted_iota(jnp.int32, (tiles, LANES), 1)
    chunk = 8
    for q0 in range(0, width, chunk):
        columns = [
            jnp.concatenate(
                [one_ref[pl.ds(q, tiles, stride=width), :], two_ref[pl.ds(q, tiles, stride=width), :]], axis=0
            )
            for q in range(q0, q0 + chunk)
        ]
        both = jnp.dot(
            left,
            jnp.concatenate(columns, axis=1),
            precision=lax.Precision.HIGHEST,
            preferred_element_type=jnp.float32,
        )
        for i in range(chunk):
            block = both[:, i * LANES : (i + 1) * LANES]
            one_ref[pl.ds(q0 + i, tiles, stride=width), :] = jnp.where(lanes < half, block[:tiles], block[tiles:])
    for t in range(tiles):
        o_ref[:, t * LANES : (t + 1) * LANES] = one_ref[t * width : (t + 1) * width, :].astype(o_ref.dtype)


def _precond(out_factor, in_factor, queries):
    width, feats = queries.shape
    rows = width * feats // LANES
    return pl.pallas_call(
        _precond_kernel,
        in_specs=[pl.BlockSpec(memory_space=pltpu.VMEM) for _ in range(3)],
        out_specs=pl.BlockSpec(memory_space=pltpu.VMEM),
        out_shape=jax.ShapeDtypeStruct((width, feats), jnp.bfloat16),
        scratch_shapes=[
            pltpu.VMEM((rows, LANES), jnp.float32),
            pltpu.VMEM((rows, LANES), jnp.float32),
            pltpu.VMEM(out_factor.shape, jnp.float32),
        ],
        compiler_params=pltpu.CompilerParams(vmem_limit_bytes=12 << 20),
        name="precond",
    )(*(pltpu.with_memory_space_constraint(x, pltpu.HBM) for x in (out_factor, in_factor, queries)))


def _joined_kernel(*refs):
    *parts, out = refs
    at = 0
    for r in parts:
        out[at : at + PANEL, :] = r[:PANEL, :]
        at += PANEL


def _joined(*parts):
    feats = parts[0].shape[1]
    return pl.pallas_call(
        _joined_kernel,
        in_specs=[pl.BlockSpec(memory_space=pltpu.VMEM) for _ in parts],
        out_specs=pl.BlockSpec(memory_space=pltpu.VMEM),
        out_shape=jax.ShapeDtypeStruct((len(parts) * PANEL, feats), parts[0].dtype),
        compiler_params=pltpu.CompilerParams(vmem_limit_bytes=4 << 20),
        name="joined",
    )(*parts)


def _score_kernel(scale, count, *refs):
    c_ref, o_ref = refs[count], refs[count + 1]
    panels = jnp.concatenate([r[...] for r in refs[:count]], axis=0)
    for i in range(c_ref.shape[0] // CBLK):
        block = slice(i * CBLK, (i + 1) * CBLK)
        part = lax.dot_general(
            panels, c_ref[block, :], (((1,), (1,)), ((), ())), preferred_element_type=jnp.float32
        )
        o_ref[:, block] = (part * scale).astype(o_ref.dtype)


def _score(pieces, flat, scale):
    rows, feats = flat.shape
    n = sum(p.shape[0] for p in pieces)
    return pl.pallas_call(
        functools.partial(_score_kernel, scale, len(pieces)),
        in_specs=[pl.BlockSpec(memory_space=pltpu.VMEM) for _ in range(len(pieces) + 1)],
        out_specs=pl.BlockSpec(memory_space=pltpu.VMEM),
        out_shape=jax.ShapeDtypeStruct((n, rows), jnp.bfloat16),
        compiler_params=pltpu.CompilerParams(vmem_limit_bytes=16 << 20),
        cost_estimate=pl.CostEstimate(
            flops=2 * n * rows * feats, bytes_accessed=2 * (rows * feats + n * feats + n * rows), transcendentals=0
        ),
        name="score",
    )(*pieces, flat)


def _place_kernel(counts, where_ref, *refs):
    out = refs[-1]
    slot = 0
    for ref, count in zip(refs[:-1], counts):
        for i in range(count):
            out[where_ref[slot]] = ref[i * PANEL : (i + 1) * PANEL, :]
            slot += 1


def _place(parts, where):
    counts = [p.shape[0] // PANEL for p in parts]
    rows = parts[0].shape[1]
    return pl.pallas_call(
        functools.partial(_place_kernel, counts),
        in_specs=[pl.BlockSpec(memory_space=pltpu.SMEM)]
        + [pl.BlockSpec(memory_space=pltpu.VMEM) for _ in parts],
        out_specs=pl.BlockSpec(memory_space=pltpu.VMEM),
        out_shape=jax.ShapeDtypeStruct((sum(counts), PANEL, rows), jnp.bfloat16),
        compiler_params=pltpu.CompilerParams(vmem_limit_bytes=12 << 20),
        name="place",
    )(where, *parts)


def _total_kernel(in_ref, o_ref):
    total = in_ref[0].astype(jnp.float32)
    for g in range(1, in_ref.shape[0]):
        total += in_ref[g].astype(jnp.float32)
    o_ref[...] = total.T


def _total(parts):
    groups, width, rows = parts.shape
    return pl.pallas_call(
        _total_kernel,
        grid=(rows // CBLK,),
        in_specs=[pl.BlockSpec((groups, width, CBLK), lambda i: (0, 0, i))],
        out_specs=pl.BlockSpec((CBLK, width), lambda i: (i, 0)),
        out_shape=jax.ShapeDtypeStruct((rows, width), jnp.float32),
        compiler_params=pltpu.CompilerParams(vmem_limit_bytes=12 << 20),
        name="total",
    )(parts)


def body(candidates, queries, out_factor, in_factor, panel_order):
    cand_rows, layer_count, features = candidates.shape
    width = queries.shape[0]
    groups = lax.axis_size("group")
    scale = 1.0 / (features * layer_count * groups) ** 0.5
    panel = _precond(out_factor[0], in_factor[0], queries.reshape(width, layer_count * features))
    flat = candidates.reshape(cand_rows, layer_count * features)

    flat = pltpu.with_memory_space_constraint(flat, pltpu.VMEM)
    me = lax.axis_index("blk")
    z, rest = me // 4, me % 4
    core = me % 2
    up = 1 - 2 * core

    sources = []

    def note(dz, dy):
        sources.append(((z + dz) % NZ) * 4 + (rest ^ (2 * dy)))
        sources.append(((z + dz) % NZ) * 4 + (rest ^ (2 * dy) ^ 1))

    def note_far(dz, dy):
        sources.append(((z + dz) % NZ) * 4 + (rest ^ (2 * dy) ^ 1))
        sources.append(((z + dz) % NZ) * 4 + (rest ^ (2 * dy)))

    note(0, 0)
    note(0, 1)
    for s in range(1, NZ // 2):
        note(-s * up, 0)
        note_far(s * up, 0)
        note(-s * up, 1)
        note_far(s * up, 1)
    for dy in (0, 1):
        sources.append(((z + NZ // 2) % NZ) * 4 + (rest ^ (2 * dy)))
        sources.append(((z + NZ // 2) % NZ) * 4 + (rest ^ (2 * dy) ^ 1))
    source = jnp.stack(sources)
    places = jnp.arange(panel_order.shape[0], dtype=jnp.int32)
    where = jnp.sum(jnp.where(panel_order[None, :] == source[:, None], places[None, :], 0), axis=1).astype(jnp.int32)

    steps = []

    across = _swap_y(panel)
    other = _swap_core(panel)
    other, where = lax.optimization_barrier((other, where))
    own, next_to = _along(panel), _along(other)
    own, next_to, across = lax.optimization_barrier((own, next_to, across))
    near = _joined(own, next_to)
    across_other = _swap_core(across)
    far = _along(_joined(across, across_other))
    pieces = [panel, other, across, across_other, near, _swap_core(near), far, _swap_core(far)]
    for s in range(2, NZ // 2 + 1):
        if s < NZ // 2:
            near, far = _along(near), _along(far)
        else:
            near, far = _along(cut), _along(_joined(far))
        if s == NZ // 2 - 1:
            cut = _joined(near)
            near, cut, pieces[0] = lax.optimization_barrier((near, cut, pieces[0]))
        elif s < NZ // 2:
            near, pieces[0] = lax.optimization_barrier((near, pieces[0]))
        steps.append(_score(pieces, flat, scale))
        steps[-1], far = lax.optimization_barrier((steps[-1], far))
        pieces = [near, _swap_core(near), far, _swap_core(far)]
    steps.append(_score(pieces, flat, scale))
    buffer = _place(steps, where).reshape(groups, -1, cand_rows)
    parts = lax.all_to_all(buffer, "group", split_axis=0, concat_axis=0, tiled=True)
    return _total(parts)


def solution(mesh):
    in_specs = (
        P("blk", "group", None),
        P("blk", "group", None),
        P("group", None, None),
        P("group", None, None),
        P(),
    )
    out_specs = P("blk", "group")
    return jax.shard_map(body, mesh=mesh, in_specs=in_specs, out_specs=out_specs, check_vma=False)
```

```python
import functools

import jax
import jax.numpy as jnp
from jax import lax
from jax.experimental import pallas as pl
from jax.experimental.pallas import tpu as pltpu
from jax.sharding import PartitionSpec as P

NZ = 8
PANEL = 32
LANES = 128
CBLK = 256


def _route(x, target):
    return lax.ppermute(x, "blk", [(i, target(*divmod(i, 4))) for i in range(NZ * 4)])


def _along(x):
    return _route(x, lambda z, rest: ((z + (1 if rest % 2 == 0 else -1)) % NZ) * 4 + rest)


def _swap_core(x):
    return _route(x, lambda z, rest: z * 4 + (rest ^ 1))


def _swap_y(x):
    return _route(x, lambda z, rest: z * 4 + (rest ^ 2))


def _precond_kernel(a_ref, b_ref, q_ref, o_ref, one_ref, two_ref, left_ref):
    width = q_ref.shape[0]
    tiles = q_ref.shape[1] // LANES
    half = LANES // 2
    zero = jnp.zeros((half, half), jnp.float32)
    b = b_ref[...]
    right = jnp.concatenate(
        [
            jnp.concatenate([b, zero, zero, b], axis=1),
            jnp.concatenate([zero, b, b, zero], axis=1),
        ],
        axis=0,
    )
    rows = jnp.concatenate([q_ref[:, t * LANES : (t + 1) * LANES] for t in range(tiles)], axis=0)
    done = None
    for _ in range(3):
        term = right.astype(jnp.bfloat16)
        right = right - term.astype(jnp.float32)
        part = jnp.dot(rows, term, preferred_element_type=jnp.float32)
        done = part if done is None else done + part
    one_ref[...] = done[:, :LANES]
    two_ref[...] = done[:, LANES:]
    row = lax.broadcasted_iota(jnp.int32, (half, half), 0)
    col = lax.broadcasted_iota(jnp.int32, (half, half), 1)
    unit = jnp.where(col < half // 2, 2 * col, 2 * (col - half // 2) + 1)
    pick = jnp.where(row == unit, 1.0, 0.0).astype(jnp.float32)
    left_ref[...] = jnp.dot(
        a_ref[...], pick, precision=lax.Precision.HIGHEST, preferred_element_type=jnp.float32
    )
    even = left_ref[pl.ds(0, half // 2, stride=2), :]
    odd = left_ref[pl.ds(1, half // 2, stride=2), :]
    odd = jnp.concatenate([odd[:, half // 2 :], odd[:, : half // 2]], axis=1)
    left = jnp.concatenate([even, odd], axis=0)
    lanes = lax.broadcasted_iota(jnp.int32, (tiles, LANES), 1)
    chunk = 8
    for q0 in range(0, width, chunk):
        columns = [
            jnp.concatenate(
                [one_ref[pl.ds(q, tiles, stride=width), :], two_ref[pl.ds(q, tiles, stride=width), :]], axis=0
            )
            for q in range(q0, q0 + chunk)
        ]
        both = jnp.dot(
            left,
            jnp.concatenate(columns, axis=1),
            precision=lax.Precision.HIGHEST,
            preferred_element_type=jnp.float32,
        )
        for i in range(chunk):
            block = both[:, i * LANES : (i + 1) * LANES]
            one_ref[pl.ds(q0 + i, tiles, stride=width), :] = jnp.where(lanes < half, block[:tiles], block[tiles:])
    for t in range(tiles):
        o_ref[:, t * LANES : (t + 1) * LANES] = one_ref[t * width : (t + 1) * width, :].astype(o_ref.dtype)


def _precond(out_factor, in_factor, queries):
    width, feats = queries.shape
    rows = width * feats // LANES
    return pl.pallas_call(
        _precond_kernel,
        in_specs=[pl.BlockSpec(memory_space=pltpu.VMEM) for _ in range(3)],
        out_specs=pl.BlockSpec(memory_space=pltpu.VMEM),
        out_shape=jax.ShapeDtypeStruct((width, feats), jnp.bfloat16),
        scratch_shapes=[
            pltpu.VMEM((rows, LANES), jnp.float32),
            pltpu.VMEM((rows, LANES), jnp.float32),
            pltpu.VMEM(out_factor.shape, jnp.float32),
        ],
        compiler_params=pltpu.CompilerParams(vmem_limit_bytes=12 << 20),
        name="precond",
    )(*(pltpu.with_memory_space_constraint(x, pltpu.HBM) for x in (out_factor, in_factor, queries)))


def _joined_kernel(*refs):
    *parts, out = refs
    at = 0
    for r in parts:
        out[at : at + PANEL, :] = r[:PANEL, :]
        at += PANEL


def _joined(*parts):
    feats = parts[0].shape[1]
    return pl.pallas_call(
        _joined_kernel,
        in_specs=[pl.BlockSpec(memory_space=pltpu.VMEM) for _ in parts],
        out_specs=pl.BlockSpec(memory_space=pltpu.VMEM),
        out_shape=jax.ShapeDtypeStruct((len(parts) * PANEL, feats), parts[0].dtype),
        compiler_params=pltpu.CompilerParams(vmem_limit_bytes=4 << 20),
        name="joined",
    )(*parts)


def _held(x):
    return pl.pallas_call(
        pltpu.sync_copy,
        in_specs=[pl.BlockSpec(memory_space=pl.ANY)],
        out_specs=pl.BlockSpec(memory_space=pltpu.VMEM),
        out_shape=pltpu.VMEM(x.shape, x.dtype),
        compiler_params=pltpu.CompilerParams(vmem_limit_bytes=1 << 20),
        cost_estimate=pl.CostEstimate(flops=0, bytes_accessed=2 * x.size * 2, transcendentals=0),
        name="held",
    )(x)


def _score_kernel(scale, count, *refs):
    c_ref, o_ref = refs[count], refs[count + 1]
    panels = jnp.concatenate([r[...] for r in refs[:count]], axis=0)
    for i in range(c_ref.shape[0] // CBLK):
        block = slice(i * CBLK, (i + 1) * CBLK)
        part = lax.dot_general(
            panels, c_ref[block, :], (((1,), (1,)), ((), ())), preferred_element_type=jnp.float32
        )
        o_ref[:, block] = (part * scale).astype(o_ref.dtype)


def _score(pieces, flat, scale):
    rows, feats = flat.shape
    n = sum(p.shape[0] for p in pieces)
    return pl.pallas_call(
        functools.partial(_score_kernel, scale, len(pieces)),
        in_specs=[pl.BlockSpec(memory_space=pltpu.VMEM) for _ in range(len(pieces) + 1)],
        out_specs=pl.BlockSpec(memory_space=pltpu.VMEM),
        out_shape=jax.ShapeDtypeStruct((n, rows), jnp.bfloat16),
        compiler_params=pltpu.CompilerParams(vmem_limit_bytes=16 << 20),
        cost_estimate=pl.CostEstimate(
            flops=2 * n * rows * feats, bytes_accessed=2 * (rows * feats + n * feats + n * rows), transcendentals=0
        ),
        name="score",
    )(*pieces, flat)


def _place_kernel(counts, where_ref, *refs):
    out = refs[-1]
    slot = 0
    for ref, count in zip(refs[:-1], counts):
        for i in range(count):
            out[where_ref[slot]] = ref[i * PANEL : (i + 1) * PANEL, :]
            slot += 1


def _place(parts, where):
    counts = [p.shape[0] // PANEL for p in parts]
    rows = parts[0].shape[1]
    return pl.pallas_call(
        functools.partial(_place_kernel, counts),
        in_specs=[pl.BlockSpec(memory_space=pltpu.SMEM)]
        + [pl.BlockSpec(memory_space=pltpu.VMEM) for _ in parts],
        out_specs=pl.BlockSpec(memory_space=pltpu.VMEM),
        out_shape=jax.ShapeDtypeStruct((where.shape[0], PANEL, rows), jnp.bfloat16),
        compiler_params=pltpu.CompilerParams(vmem_limit_bytes=12 << 20),
        name="place",
    )(where, *parts)


def _finish_kernel(scale, count, where_ref, *refs):
    c_ref, o_ref = refs[count], refs[count + 2]
    first = where_ref.shape[0] - count
    panels = jnp.concatenate([r[...] for r in refs[:count]], axis=0)
    for i in range(c_ref.shape[0] // CBLK):
        block = slice(i * CBLK, (i + 1) * CBLK)
        part = lax.dot_general(
            panels, c_ref[block, :], (((1,), (1,)), ((), ())), preferred_element_type=jnp.float32
        )
        part = (part * scale).astype(o_ref.dtype)
        for j in range(count):
            o_ref[where_ref[first + j], :, block] = part[j * PANEL : (j + 1) * PANEL, :]


def _finish(pieces, flat, scale, where, early):
    rows, feats = flat.shape
    n = len(pieces) * PANEL
    return pl.pallas_call(
        functools.partial(_finish_kernel, scale, len(pieces)),
        in_specs=[pl.BlockSpec(memory_space=pltpu.SMEM)]
        + [pl.BlockSpec(memory_space=pltpu.VMEM) for _ in range(len(pieces) + 2)],
        out_specs=pl.BlockSpec(memory_space=pltpu.VMEM),
        out_shape=jax.ShapeDtypeStruct(early.shape, early.dtype),
        input_output_aliases={len(pieces) + 2: 0},
        compiler_params=pltpu.CompilerParams(vmem_limit_bytes=16 << 20),
        cost_estimate=pl.CostEstimate(
            flops=2 * n * rows * feats, bytes_accessed=2 * (rows * feats + n * feats + n * rows), transcendentals=0
        ),
        name="finish",
    )(where, *pieces, flat, early)


def _total_kernel(in_ref, o_ref):
    width = in_ref.shape[1]
    for i in range(in_ref.shape[2] // width):
        block = slice(i * width, (i + 1) * width)
        total = in_ref[0, :, block].astype(jnp.float32)
        for g in range(1, in_ref.shape[0]):
            total += in_ref[g, :, block].astype(jnp.float32)
        o_ref[block, :] = total.T


def _total(parts):
    groups, width, rows = parts.shape
    return pl.pallas_call(
        _total_kernel,
        in_specs=[pl.BlockSpec(memory_space=pltpu.VMEM)],
        out_specs=pl.BlockSpec(memory_space=pltpu.VMEM),
        out_shape=jax.ShapeDtypeStruct((rows, width), jnp.float32),
        compiler_params=pltpu.CompilerParams(vmem_limit_bytes=12 << 20),
        name="total",
    )(parts)


def body(candidates, queries, out_factor, in_factor, panel_order):
    cand_rows, layer_count, features = candidates.shape
    width = queries.shape[0]
    groups = lax.axis_size("group")
    scale = 1.0 / (features * layer_count * groups) ** 0.5
    panel = _precond(out_factor[0], in_factor[0], queries.reshape(width, layer_count * features))
    flat = candidates.reshape(cand_rows, layer_count * features)

    me = lax.axis_index("blk")
    z, rest = me // 4, me % 4
    core = me % 2
    up = 1 - 2 * core

    sources = []

    def note(dz, dy):
        sources.append(((z + dz) % NZ) * 4 + (rest ^ (2 * dy)))
        sources.append(((z + dz) % NZ) * 4 + (rest ^ (2 * dy) ^ 1))

    def note_far(dz, dy):
        sources.append(((z + dz) % NZ) * 4 + (rest ^ (2 * dy) ^ 1))
        sources.append(((z + dz) % NZ) * 4 + (rest ^ (2 * dy)))

    note(0, 0)
    note(0, 1)
    for s in range(1, NZ // 2):
        note(-s * up, 0)
        note_far(s * up, 0)
        note(-s * up, 1)
        note_far(s * up, 1)
    for dy in (0, 1):
        sources.append(((z + NZ // 2) % NZ) * 4 + (rest ^ (2 * dy)))
        sources.append(((z + NZ // 2) % NZ) * 4 + (rest ^ (2 * dy) ^ 1))
    source = jnp.stack(sources)
    places = jnp.arange(panel_order.shape[0], dtype=jnp.int32)
    where = jnp.sum(jnp.where(panel_order[None, :] == source[:, None], places[None, :], 0), axis=1).astype(jnp.int32)

    steps = []

    across = _swap_y(panel)
    other = _swap_core(panel)
    other, where = lax.optimization_barrier((other, where))
    own, next_to = _along(panel), _along(other)
    flat = _held(pltpu.with_memory_space_constraint(flat, pltpu.HBM))
    own, next_to, across, flat = lax.optimization_barrier((own, next_to, across, flat))
    near = _joined(own, next_to)
    across_other = _swap_core(across)
    far = _along(_joined(across, across_other))
    pieces = [panel, other, across, across_other, near, _swap_core(near), far, _swap_core(far)]
    for s in range(2, NZ // 2):
        near, far = _along(near), _along(far)
        cut = _joined(near)
        near, cut, pieces[0] = lax.optimization_barrier((near, cut, pieces[0]))
        steps.append(_score(pieces, flat, scale))
        if s == NZ // 2 - 1:
            steps[-1], last = lax.optimization_barrier((steps[-1], _along(cut)))
            last, far = lax.optimization_barrier((last, far))
        steps[-1], far = lax.optimization_barrier((steps[-1], far))
        pieces = [near, _swap_core(near), far, _swap_core(far)]
    beyond = _along(_joined(far))
    steps.append(_score(pieces, flat, scale))
    early = _place(steps, where)
    early, beyond = lax.optimization_barrier((early, beyond))
    buffer = _finish([last, _swap_core(last), beyond, _swap_core(beyond)], flat, scale, where, early)
    buffer = buffer.reshape(groups, -1, cand_rows)
    parts = lax.all_to_all(buffer, "group", split_axis=0, concat_axis=0, tiled=True)
    return _total(parts)


def solution(mesh):
    in_specs = (
        P("blk", "group", None),
        P("blk", "group", None),
        P("group", None, None),
        P("group", None, None),
        P(),
    )
    out_specs = P("blk", "group")
    return jax.shard_map(body, mesh=mesh, in_specs=in_specs, out_specs=out_specs, check_vma=False)
```

```python
import functools

import jax
import jax.numpy as jnp
from jax import lax
from jax.experimental import pallas as pl
from jax.experimental.pallas import tpu as pltpu
from jax.sharding import PartitionSpec as P

NZ = 8
PANEL = 32
LANES = 128
CBLK = 256


def _route(x, target):
    return lax.ppermute(x, "blk", [(i, target(*divmod(i, 4))) for i in range(NZ * 4)])


def _along(x):
    return _route(x, lambda z, rest: ((z + (1 if rest % 2 == 0 else -1)) % NZ) * 4 + rest)


def _swap_core(x):
    return _route(x, lambda z, rest: z * 4 + (rest ^ 1))


def _swap_y(x):
    return _route(x, lambda z, rest: z * 4 + (rest ^ 2))


def _precond_kernel(a_ref, b_ref, q_ref, o_ref, one_ref, two_ref, left_ref):
    width = q_ref.shape[0]
    tiles = q_ref.shape[1] // LANES
    half = LANES // 2
    zero = jnp.zeros((half, half), jnp.float32)
    b = b_ref[...]
    right = jnp.concatenate(
        [
            jnp.concatenate([b, zero, zero, b], axis=1),
            jnp.concatenate([zero, b, b, zero], axis=1),
        ],
        axis=0,
    )
    rows = jnp.concatenate([q_ref[:, t * LANES : (t + 1) * LANES] for t in range(tiles)], axis=0)
    done = None
    for _ in range(3):
        term = right.astype(jnp.bfloat16)
        right = right - term.astype(jnp.float32)
        part = jnp.dot(rows, term, preferred_element_type=jnp.float32)
        done = part if done is None else done + part
    one_ref[...] = done[:, :LANES]
    two_ref[...] = done[:, LANES:]
    row = lax.broadcasted_iota(jnp.int32, (half, half), 0)
    col = lax.broadcasted_iota(jnp.int32, (half, half), 1)
    unit = jnp.where(col < half // 2, 2 * col, 2 * (col - half // 2) + 1)
    pick = jnp.where(row == unit, 1.0, 0.0).astype(jnp.float32)
    left_ref[...] = jnp.dot(
        a_ref[...], pick, precision=lax.Precision.HIGHEST, preferred_element_type=jnp.float32
    )
    even = left_ref[pl.ds(0, half // 2, stride=2), :]
    odd = left_ref[pl.ds(1, half // 2, stride=2), :]
    odd = jnp.concatenate([odd[:, half // 2 :], odd[:, : half // 2]], axis=1)
    left = jnp.concatenate([even, odd], axis=0)
    lanes = lax.broadcasted_iota(jnp.int32, (tiles, LANES), 1)
    chunk = 8
    for q0 in range(0, width, chunk):
        columns = [
            jnp.concatenate(
                [one_ref[pl.ds(q, tiles, stride=width), :], two_ref[pl.ds(q, tiles, stride=width), :]], axis=0
            )
            for q in range(q0, q0 + chunk)
        ]
        both = jnp.dot(
            left,
            jnp.concatenate(columns, axis=1),
            precision=lax.Precision.HIGHEST,
            preferred_element_type=jnp.float32,
        )
        for i in range(chunk):
            block = both[:, i * LANES : (i + 1) * LANES]
            one_ref[pl.ds(q0 + i, tiles, stride=width), :] = jnp.where(lanes < half, block[:tiles], block[tiles:])
    for t in range(tiles):
        o_ref[:, t * LANES : (t + 1) * LANES] = one_ref[t * width : (t + 1) * width, :].astype(o_ref.dtype)


def _precond(out_factor, in_factor, queries):
    width, feats = queries.shape
    rows = width * feats // LANES
    return pl.pallas_call(
        _precond_kernel,
        in_specs=[pl.BlockSpec(memory_space=pltpu.VMEM) for _ in range(3)],
        out_specs=pl.BlockSpec(memory_space=pltpu.VMEM),
        out_shape=jax.ShapeDtypeStruct((width, feats), jnp.bfloat16),
        scratch_shapes=[
            pltpu.VMEM((rows, LANES), jnp.float32),
            pltpu.VMEM((rows, LANES), jnp.float32),
            pltpu.VMEM(out_factor.shape, jnp.float32),
        ],
        compiler_params=pltpu.CompilerParams(vmem_limit_bytes=12 << 20),
        name="precond",
    )(*(pltpu.with_memory_space_constraint(x, pltpu.HBM) for x in (out_factor, in_factor, queries)))


def _joined_kernel(*refs):
    *parts, out = refs
    at = 0
    for r in parts:
        out[at : at + PANEL, :] = r[:PANEL, :]
        at += PANEL


def _joined(*parts):
    feats = parts[0].shape[1]
    return pl.pallas_call(
        _joined_kernel,
        in_specs=[pl.BlockSpec(memory_space=pltpu.VMEM) for _ in parts],
        out_specs=pl.BlockSpec(memory_space=pltpu.VMEM),
        out_shape=jax.ShapeDtypeStruct((len(parts) * PANEL, feats), parts[0].dtype),
        compiler_params=pltpu.CompilerParams(vmem_limit_bytes=4 << 20),
        name="joined",
    )(*parts)


def _held(x):
    return pl.pallas_call(
        pltpu.sync_copy,
        in_specs=[pl.BlockSpec(memory_space=pl.ANY)],
        out_specs=pl.BlockSpec(memory_space=pltpu.VMEM),
        out_shape=pltpu.VMEM(x.shape, x.dtype),
        compiler_params=pltpu.CompilerParams(vmem_limit_bytes=1 << 20),
        cost_estimate=pl.CostEstimate(flops=0, bytes_accessed=2 * x.size * 2, transcendentals=0),
        name="held",
    )(x)


def _score_kernel(scale, count, *refs):
    c_ref, o_ref = refs[count], refs[count + 1]
    panels = jnp.concatenate([r[...] for r in refs[:count]], axis=0)
    for i in range(c_ref.shape[0] // CBLK):
        block = slice(i * CBLK, (i + 1) * CBLK)
        part = lax.dot_general(
            panels, c_ref[block, :], (((1,), (1,)), ((), ())), preferred_element_type=jnp.float32
        )
        o_ref[:, block] = (part * scale).astype(o_ref.dtype)


def _score(pieces, flat, scale):
    rows, feats = flat.shape
    n = sum(p.shape[0] for p in pieces)
    return pl.pallas_call(
        functools.partial(_score_kernel, scale, len(pieces)),
        in_specs=[pl.BlockSpec(memory_space=pltpu.VMEM) for _ in range(len(pieces) + 1)],
        out_specs=pl.BlockSpec(memory_space=pltpu.VMEM),
        out_shape=jax.ShapeDtypeStruct((n, rows), jnp.bfloat16),
        compiler_params=pltpu.CompilerParams(vmem_limit_bytes=16 << 20),
        cost_estimate=pl.CostEstimate(
            flops=2 * n * rows * feats, bytes_accessed=2 * (rows * feats + n * feats + n * rows), transcendentals=0
        ),
        name="score",
    )(*pieces, flat)


def _place_kernel(counts, where_ref, *refs):
    out = refs[-1]
    slot = 0
    for ref, count in zip(refs[:-1], counts):
        for i in range(count):
            out[where_ref[slot]] = ref[i * PANEL : (i + 1) * PANEL, :]
            slot += 1


def _place(parts, where):
    counts = [p.shape[0] // PANEL for p in parts]
    rows = parts[0].shape[1]
    return pl.pallas_call(
        functools.partial(_place_kernel, counts),
        in_specs=[pl.BlockSpec(memory_space=pltpu.SMEM)]
        + [pl.BlockSpec(memory_space=pltpu.VMEM) for _ in parts],
        out_specs=pl.BlockSpec(memory_space=pltpu.VMEM),
        out_shape=jax.ShapeDtypeStruct((where.shape[0], PANEL, rows), jnp.bfloat16),
        compiler_params=pltpu.CompilerParams(vmem_limit_bytes=12 << 20),
        name="place",
    )(where, *parts)


def _finish_kernel(scale, count, where_ref, *refs):
    c_ref, o_ref = refs[count], refs[count + 2]
    first = where_ref.shape[0] - count
    panels = jnp.concatenate([r[...] for r in refs[:count]], axis=0)
    for i in range(c_ref.shape[0] // CBLK):
        block = slice(i * CBLK, (i + 1) * CBLK)
        part = lax.dot_general(
            panels, c_ref[block, :], (((1,), (1,)), ((), ())), preferred_element_type=jnp.float32
        )
        part = (part * scale).astype(o_ref.dtype)
        for j in range(count):
            o_ref[where_ref[first + j], :, block] = part[j * PANEL : (j + 1) * PANEL, :]


def _finish(pieces, flat, scale, where, early):
    rows, feats = flat.shape
    n = len(pieces) * PANEL
    return pl.pallas_call(
        functools.partial(_finish_kernel, scale, len(pieces)),
        in_specs=[pl.BlockSpec(memory_space=pltpu.SMEM)]
        + [pl.BlockSpec(memory_space=pltpu.VMEM) for _ in range(len(pieces) + 2)],
        out_specs=pl.BlockSpec(memory_space=pltpu.VMEM),
        out_shape=jax.ShapeDtypeStruct(early.shape, early.dtype),
        input_output_aliases={len(pieces) + 2: 0},
        compiler_params=pltpu.CompilerParams(vmem_limit_bytes=16 << 20),
        cost_estimate=pl.CostEstimate(
            flops=2 * n * rows * feats, bytes_accessed=2 * (rows * feats + n * feats + n * rows), transcendentals=0
        ),
        name="finish",
    )(where, *pieces, flat, early)


def _total_kernel(in_ref, o_ref):
    width = in_ref.shape[1]
    for i in range(in_ref.shape[2] // width):
        block = slice(i * width, (i + 1) * width)
        total = in_ref[0, :, block].astype(jnp.float32)
        for g in range(1, in_ref.shape[0]):
            total += in_ref[g, :, block].astype(jnp.float32)
        o_ref[block, :] = total.T


def _total(parts):
    groups, width, rows = parts.shape
    return pl.pallas_call(
        _total_kernel,
        in_specs=[pl.BlockSpec(memory_space=pltpu.VMEM)],
        out_specs=pl.BlockSpec(memory_space=pltpu.VMEM),
        out_shape=jax.ShapeDtypeStruct((rows, width), jnp.float32),
        compiler_params=pltpu.CompilerParams(vmem_limit_bytes=12 << 20),
        name="total",
    )(parts)


def body(candidates, queries, out_factor, in_factor, panel_order):
    cand_rows, layer_count, features = candidates.shape
    width = queries.shape[0]
    groups = lax.axis_size("group")
    scale = 1.0 / (features * layer_count * groups) ** 0.5
    panel = _precond(out_factor[0], in_factor[0], queries.reshape(width, layer_count * features))
    flat = candidates.reshape(cand_rows, layer_count * features)

    me = lax.axis_index("blk")
    z, rest = me // 4, me % 4
    core = me % 2
    up = 1 - 2 * core

    sources = []

    def note(dz, dy):
        sources.append(((z + dz) % NZ) * 4 + (rest ^ (2 * dy)))
        sources.append(((z + dz) % NZ) * 4 + (rest ^ (2 * dy) ^ 1))

    def note_far(dz, dy):
        sources.append(((z + dz) % NZ) * 4 + (rest ^ (2 * dy) ^ 1))
        sources.append(((z + dz) % NZ) * 4 + (rest ^ (2 * dy)))

    note(0, 0)
    note(0, 1)
    for s in range(1, NZ // 2):
        note(-s * up, 0)
        note_far(s * up, 0)
        note(-s * up, 1)
        note_far(s * up, 1)
    for dy in (0, 1):
        sources.append(((z + NZ // 2) % NZ) * 4 + (rest ^ (2 * dy)))
        sources.append(((z + NZ // 2) % NZ) * 4 + (rest ^ (2 * dy) ^ 1))
    source = jnp.stack(sources)
    places = jnp.arange(panel_order.shape[0], dtype=jnp.int32)
    where = jnp.sum(jnp.where(panel_order[None, :] == source[:, None], places[None, :], 0), axis=1).astype(jnp.int32)

    steps = []

    other = _swap_core(panel)
    other, sent = lax.optimization_barrier((other, panel))
    across = _swap_y(sent)
    own, next_to = _along(panel), _along(other)
    flat, where = lax.optimization_barrier((flat, where))
    flat = _held(pltpu.with_memory_space_constraint(flat, pltpu.HBM))
    near = _joined(own, next_to)
    near, across, flat = lax.optimization_barrier((near, across, flat))
    across_other = _swap_core(across)
    far = _along(_joined(across, across_other))
    pieces = [panel, other, across, across_other, near, _swap_core(near), far, _swap_core(far)]
    for s in range(2, NZ // 2):
        near, far = _along(near), _along(far)
        cut = _joined(near)
        near, cut, pieces[0] = lax.optimization_barrier((near, cut, pieces[0]))
        steps.append(_score(pieces, flat, scale))
        if s == NZ // 2 - 1:
            steps[-1], last = lax.optimization_barrier((steps[-1], _along(cut)))
            last, far = lax.optimization_barrier((last, far))
        steps[-1], far = lax.optimization_barrier((steps[-1], far))
        pieces = [near, _swap_core(near), far, _swap_core(far)]
    beyond = _along(_joined(far))
    steps.append(_score(pieces, flat, scale))
    early = _place(steps, where)
    early, beyond = lax.optimization_barrier((early, beyond))
    buffer = _finish([last, _swap_core(last), beyond, _swap_core(beyond)], flat, scale, where, early)
    buffer = buffer.reshape(groups, -1, cand_rows)
    parts = lax.all_to_all(buffer, "group", split_axis=0, concat_axis=0, tiled=True)
    return _total(parts)


def solution(mesh):
    in_specs = (
        P("blk", "group", None),
        P("blk", "group", None),
        P("group", None, None),
        P("group", None, None),
        P(),
    )
    out_specs = P("blk", "group")
    return jax.shard_map(body, mesh=mesh, in_specs=in_specs, out_specs=out_specs, check_vma=False)
```

```python
import functools

import jax
import jax.numpy as jnp
from jax import lax
from jax.experimental import pallas as pl
from jax.experimental.pallas import tpu as pltpu
from jax.sharding import PartitionSpec as P

NZ = 8
PANEL = 32
LANES = 128
CBLK = 256


def _route(x, target):
    return lax.ppermute(x, "blk", [(i, target(*divmod(i, 4))) for i in range(NZ * 4)])


def _along(x):
    return _route(x, lambda z, rest: ((z + (1 if rest % 2 == 0 else -1)) % NZ) * 4 + rest)


def _swap_core(x):
    return _route(x, lambda z, rest: z * 4 + (rest ^ 1))


def _swap_y(x):
    return _route(x, lambda z, rest: z * 4 + (rest ^ 2))


def _precond_kernel(a_ref, b_ref, q_ref, o_ref, one_ref, two_ref, left_ref):
    width = q_ref.shape[0]
    tiles = q_ref.shape[1] // LANES
    half = LANES // 2
    zero = jnp.zeros((half, half), jnp.float32)
    b = b_ref[...]
    right = jnp.concatenate(
        [
            jnp.concatenate([b, zero, zero, b], axis=1),
            jnp.concatenate([zero, b, b, zero], axis=1),
        ],
        axis=0,
    )
    rows = jnp.concatenate([q_ref[:, t * LANES : (t + 1) * LANES] for t in range(tiles)], axis=0)
    done = None
    for _ in range(3):
        term = right.astype(jnp.bfloat16)
        right = right - term.astype(jnp.float32)
        part = jnp.dot(rows, term, preferred_element_type=jnp.float32)
        done = part if done is None else done + part
    one_ref[...] = done[:, :LANES]
    two_ref[...] = done[:, LANES:]
    row = lax.broadcasted_iota(jnp.int32, (half, half), 0)
    col = lax.broadcasted_iota(jnp.int32, (half, half), 1)
    unit = jnp.where(col < half // 2, 2 * col, 2 * (col - half // 2) + 1)
    pick = jnp.where(row == unit, 1.0, 0.0).astype(jnp.float32)
    left_ref[...] = jnp.dot(
        a_ref[...], pick, precision=lax.Precision.HIGHEST, preferred_element_type=jnp.float32
    )
    even = left_ref[pl.ds(0, half // 2, stride=2), :]
    odd = left_ref[pl.ds(1, half // 2, stride=2), :]
    odd = jnp.concatenate([odd[:, half // 2 :], odd[:, : half // 2]], axis=1)
    left = jnp.concatenate([even, odd], axis=0)
    lanes = lax.broadcasted_iota(jnp.int32, (tiles, LANES), 1)
    chunk = 8
    for q0 in range(0, width, chunk):
        columns = [
            jnp.concatenate(
                [one_ref[pl.ds(q, tiles, stride=width), :], two_ref[pl.ds(q, tiles, stride=width), :]], axis=0
            )
            for q in range(q0, q0 + chunk)
        ]
        both = jnp.dot(
            left,
            jnp.concatenate(columns, axis=1),
            precision=lax.Precision.HIGHEST,
            preferred_element_type=jnp.float32,
        )
        for i in range(chunk):
            block = both[:, i * LANES : (i + 1) * LANES]
            one_ref[pl.ds(q0 + i, tiles, stride=width), :] = jnp.where(lanes < half, block[:tiles], block[tiles:])
    for t in range(tiles):
        o_ref[:, t * LANES : (t + 1) * LANES] = one_ref[t * width : (t + 1) * width, :].astype(o_ref.dtype)


def _precond(out_factor, in_factor, queries):
    width, feats = queries.shape
    rows = width * feats // LANES
    return pl.pallas_call(
        _precond_kernel,
        in_specs=[pl.BlockSpec(memory_space=pltpu.VMEM) for _ in range(3)],
        out_specs=pl.BlockSpec(memory_space=pltpu.VMEM),
        out_shape=jax.ShapeDtypeStruct((width, feats), jnp.bfloat16),
        scratch_shapes=[
            pltpu.VMEM((rows, LANES), jnp.float32),
            pltpu.VMEM((rows, LANES), jnp.float32),
            pltpu.VMEM(out_factor.shape, jnp.float32),
        ],
        compiler_params=pltpu.CompilerParams(vmem_limit_bytes=12 << 20),
        name="precond",
    )(*(pltpu.with_memory_space_constraint(x, pltpu.HBM) for x in (out_factor, in_factor, queries)))


def _joined_kernel(*refs):
    *parts, out = refs
    at = 0
    for r in parts:
        out[at : at + PANEL, :] = r[:PANEL, :]
        at += PANEL


def _joined(*parts):
    feats = parts[0].shape[1]
    return pl.pallas_call(
        _joined_kernel,
        in_specs=[pl.BlockSpec(memory_space=pltpu.VMEM) for _ in parts],
        out_specs=pl.BlockSpec(memory_space=pltpu.VMEM),
        out_shape=jax.ShapeDtypeStruct((len(parts) * PANEL, feats), parts[0].dtype),
        compiler_params=pltpu.CompilerParams(vmem_limit_bytes=4 << 20),
        name="joined",
    )(*parts)


def _held(x):
    return pl.pallas_call(
        pltpu.sync_copy,
        in_specs=[pl.BlockSpec(memory_space=pl.ANY)],
        out_specs=pl.BlockSpec(memory_space=pltpu.VMEM),
        out_shape=pltpu.VMEM(x.shape, x.dtype),
        compiler_params=pltpu.CompilerParams(vmem_limit_bytes=1 << 20),
        cost_estimate=pl.CostEstimate(flops=0, bytes_accessed=2 * x.size * 2, transcendentals=0),
        name="held",
    )(x)


def _score_kernel(scale, count, *refs):
    c_ref, o_ref = refs[count], refs[count + 1]
    panels = jnp.concatenate([r[...] for r in refs[:count]], axis=0)
    for i in range(c_ref.shape[0] // CBLK):
        block = slice(i * CBLK, (i + 1) * CBLK)
        part = lax.dot_general(
            panels, c_ref[block, :], (((1,), (1,)), ((), ())), preferred_element_type=jnp.float32
        )
        o_ref[:, block] = (part * scale).astype(o_ref.dtype)


def _score(pieces, flat, scale):
    rows, feats = flat.shape
    n = sum(p.shape[0] for p in pieces)
    return pl.pallas_call(
        functools.partial(_score_kernel, scale, len(pieces)),
        in_specs=[pl.BlockSpec(memory_space=pltpu.VMEM) for _ in range(len(pieces) + 1)],
        out_specs=pl.BlockSpec(memory_space=pltpu.VMEM),
        out_shape=jax.ShapeDtypeStruct((n, rows), jnp.bfloat16),
        compiler_params=pltpu.CompilerParams(vmem_limit_bytes=16 << 20),
        cost_estimate=pl.CostEstimate(
            flops=2 * n * rows * feats, bytes_accessed=2 * (rows * feats + n * feats + n * rows), transcendentals=0
        ),
        name="score",
    )(*pieces, flat)


def _place_kernel(counts, where_ref, *refs):
    out = refs[-1]
    slot = 0
    for ref, count in zip(refs[:-1], counts):
        for i in range(count):
            out[where_ref[slot]] = ref[i * PANEL : (i + 1) * PANEL, :]
            slot += 1


def _place(parts, where):
    counts = [p.shape[0] // PANEL for p in parts]
    rows = parts[0].shape[1]
    return pl.pallas_call(
        functools.partial(_place_kernel, counts),
        in_specs=[pl.BlockSpec(memory_space=pltpu.SMEM)]
        + [pl.BlockSpec(memory_space=pltpu.VMEM) for _ in parts],
        out_specs=pl.BlockSpec(memory_space=pltpu.VMEM),
        out_shape=jax.ShapeDtypeStruct((where.shape[0], PANEL, rows), jnp.bfloat16),
        compiler_params=pltpu.CompilerParams(vmem_limit_bytes=12 << 20),
        name="place",
    )(where, *parts)


def _finish_kernel(scale, count, where_ref, *refs):
    c_ref, o_ref = refs[count], refs[count + 2]
    first = where_ref.shape[0] - count
    panels = jnp.concatenate([r[...] for r in refs[:count]], axis=0)
    for i in range(c_ref.shape[0] // CBLK):
        block = slice(i * CBLK, (i + 1) * CBLK)
        part = lax.dot_general(
            c_ref[block, :], panels, (((1,), (1,)), ((), ())), preferred_element_type=jnp.float32
        )
        part = (part * scale).T.astype(o_ref.dtype)
        for j in range(count):
            o_ref[where_ref[first + j], :, block] = part[j * PANEL : (j + 1) * PANEL, :]


def _finish(pieces, flat, scale, where, early):
    rows, feats = flat.shape
    n = len(pieces) * PANEL
    return pl.pallas_call(
        functools.partial(_finish_kernel, scale, len(pieces)),
        in_specs=[pl.BlockSpec(memory_space=pltpu.SMEM)]
        + [pl.BlockSpec(memory_space=pltpu.VMEM) for _ in range(len(pieces) + 2)],
        out_specs=pl.BlockSpec(memory_space=pltpu.VMEM),
        out_shape=jax.ShapeDtypeStruct(early.shape, early.dtype),
        input_output_aliases={len(pieces) + 2: 0},
        compiler_params=pltpu.CompilerParams(vmem_limit_bytes=16 << 20),
        cost_estimate=pl.CostEstimate(
            flops=2 * n * rows * feats, bytes_accessed=2 * (rows * feats + n * feats + n * rows), transcendentals=0
        ),
        name="finish",
    )(where, *pieces, flat, early)


def _total_kernel(in_ref, o_ref):
    width = in_ref.shape[1]
    for i in range(in_ref.shape[2] // width):
        block = slice(i * width, (i + 1) * width)
        total = in_ref[0, :, block].astype(jnp.float32)
        for g in range(1, in_ref.shape[0]):
            total += in_ref[g, :, block].astype(jnp.float32)
        o_ref[block, :] = total.T


def _total(parts):
    groups, width, rows = parts.shape
    return pl.pallas_call(
        _total_kernel,
        in_specs=[pl.BlockSpec(memory_space=pltpu.VMEM)],
        out_specs=pl.BlockSpec(memory_space=pltpu.VMEM),
        out_shape=jax.ShapeDtypeStruct((rows, width), jnp.float32),
        compiler_params=pltpu.CompilerParams(vmem_limit_bytes=12 << 20),
        name="total",
    )(parts)


def body(candidates, queries, out_factor, in_factor, panel_order):
    cand_rows, layer_count, features = candidates.shape
    width = queries.shape[0]
    groups = lax.axis_size("group")
    scale = 1.0 / (features * layer_count * groups) ** 0.5
    panel = _precond(out_factor[0], in_factor[0], queries.reshape(width, layer_count * features))
    flat = candidates.reshape(cand_rows, layer_count * features)

    me = lax.axis_index("blk")
    z, rest = me // 4, me % 4
    core = me % 2
    up = 1 - 2 * core

    sources = []

    def note(dz, dy):
        sources.append(((z + dz) % NZ) * 4 + (rest ^ (2 * dy)))
        sources.append(((z + dz) % NZ) * 4 + (rest ^ (2 * dy) ^ 1))

    def note_far(dz, dy):
        sources.append(((z + dz) % NZ) * 4 + (rest ^ (2 * dy) ^ 1))
        sources.append(((z + dz) % NZ) * 4 + (rest ^ (2 * dy)))

    note(0, 0)
    note(0, 1)
    for s in range(1, NZ // 2):
        note(-s * up, 0)
        note_far(s * up, 0)
        note(-s * up, 1)
        note_far(s * up, 1)
    for dy in (0, 1):
        sources.append(((z + NZ // 2) % NZ) * 4 + (rest ^ (2 * dy)))
        sources.append(((z + NZ // 2) % NZ) * 4 + (rest ^ (2 * dy) ^ 1))
    source = jnp.stack(sources)
    places = jnp.arange(panel_order.shape[0], dtype=jnp.int32)
    where = jnp.sum(jnp.where(panel_order[None, :] == source[:, None], places[None, :], 0), axis=1).astype(jnp.int32)

    steps = []

    other = _swap_core(panel)
    other, sent = lax.optimization_barrier((other, panel))
    across = _swap_y(sent)
    own, next_to = _along(panel), _along(other)
    flat, where = lax.optimization_barrier((flat, where))
    flat = _held(pltpu.with_memory_space_constraint(flat, pltpu.HBM))
    near = _joined(own, next_to)
    near, across, flat = lax.optimization_barrier((near, across, flat))
    across_other = _swap_core(across)
    far = _along(_joined(across, across_other))
    pieces = [panel, other, across, across_other, near, _swap_core(near), far, _swap_core(far)]
    for s in range(2, NZ // 2):
        near, far = _along(near), _along(far)
        cut = _joined(near)
        near, cut, pieces[0] = lax.optimization_barrier((near, cut, pieces[0]))
        steps.append(_score(pieces, flat, scale))
        if s == NZ // 2 - 1:
            steps[-1], last = lax.optimization_barrier((steps[-1], _along(cut)))
            last, far = lax.optimization_barrier((last, far))
        steps[-1], far = lax.optimization_barrier((steps[-1], far))
        pieces = [near, _swap_core(near), far, _swap_core(far)]
    beyond = _along(_joined(far))
    steps.append(_score(pieces, flat, scale))
    early = _place(steps, where)
    early, beyond = lax.optimization_barrier((early, beyond))
    buffer = _finish([last, _swap_core(last), beyond, _swap_core(beyond)], flat, scale, where, early)
    buffer = buffer.reshape(groups, -1, cand_rows)
    parts = lax.all_to_all(buffer, "group", split_axis=0, concat_axis=0, tiled=True)
    return _total(parts)


def solution(mesh):
    in_specs = (
        P("blk", "group", None),
        P("blk", "group", None),
        P("group", None, None),
        P("group", None, None),
        P(),
    )
    out_specs = P("blk", "group")
    return jax.shard_map(body, mesh=mesh, in_specs=in_specs, out_specs=out_specs, check_vma=False)
```

```python
import functools

import jax
import jax.numpy as jnp
from jax import lax
from jax.experimental import pallas as pl
from jax.experimental.pallas import tpu as pltpu
from jax.sharding import PartitionSpec as P

NZ = 8
PANEL = 32
LANES = 128
CBLK = 256


def _route(x, target):
    return lax.ppermute(x, "blk", [(i, target(*divmod(i, 4))) for i in range(NZ * 4)])


def _along(x):
    return _route(x, lambda z, rest: ((z + (1 if rest % 2 == 0 else -1)) % NZ) * 4 + rest)


def _swap_core(x):
    return _route(x, lambda z, rest: z * 4 + (rest ^ 1))


def _swap_y(x):
    return _route(x, lambda z, rest: z * 4 + (rest ^ 2))


def _precond_kernel(a_ref, b_ref, q_ref, o_ref, one_ref, two_ref, left_ref):
    width = q_ref.shape[0]
    tiles = q_ref.shape[1] // LANES
    half = LANES // 2
    zero = jnp.zeros((half, half), jnp.float32)
    b = b_ref[...]
    right = jnp.concatenate(
        [
            jnp.concatenate([b, zero, zero, b], axis=1),
            jnp.concatenate([zero, b, b, zero], axis=1),
        ],
        axis=0,
    )
    rows = jnp.concatenate([q_ref[:, t * LANES : (t + 1) * LANES] for t in range(tiles)], axis=0)
    done = None
    for _ in range(3):
        term = right.astype(jnp.bfloat16)
        right = right - term.astype(jnp.float32)
        part = jnp.dot(rows, term, preferred_element_type=jnp.float32)
        done = part if done is None else done + part
    one_ref[...] = done[:, :LANES]
    two_ref[...] = done[:, LANES:]
    row = lax.broadcasted_iota(jnp.int32, (half, half), 0)
    col = lax.broadcasted_iota(jnp.int32, (half, half), 1)
    unit = jnp.where(col < half // 2, 2 * col, 2 * (col - half // 2) + 1)
    pick = jnp.where(row == unit, 1.0, 0.0).astype(jnp.float32)
    left_ref[...] = jnp.dot(
        a_ref[...], pick, precision=lax.Precision.HIGHEST, preferred_element_type=jnp.float32
    )
    even = left_ref[pl.ds(0, half // 2, stride=2), :]
    odd = left_ref[pl.ds(1, half // 2, stride=2), :]
    odd = jnp.concatenate([odd[:, half // 2 :], odd[:, : half // 2]], axis=1)
    left = jnp.concatenate([even, odd], axis=0)
    lanes = lax.broadcasted_iota(jnp.int32, (tiles, LANES), 1)
    chunk = 8
    for q0 in range(0, width, chunk):
        columns = [
            jnp.concatenate(
                [one_ref[pl.ds(q, tiles, stride=width), :], two_ref[pl.ds(q, tiles, stride=width), :]], axis=0
            )
            for q in range(q0, q0 + chunk)
        ]
        both = jnp.dot(
            left,
            jnp.concatenate(columns, axis=1),
            precision=lax.Precision.HIGHEST,
            preferred_element_type=jnp.float32,
        )
        for i in range(chunk):
            block = both[:, i * LANES : (i + 1) * LANES]
            one_ref[pl.ds(q0 + i, tiles, stride=width), :] = jnp.where(lanes < half, block[:tiles], block[tiles:])
    for t in range(tiles):
        o_ref[:, t * LANES : (t + 1) * LANES] = one_ref[t * width : (t + 1) * width, :].astype(o_ref.dtype)


def _precond(out_factor, in_factor, queries):
    width, feats = queries.shape
    rows = width * feats // LANES
    return pl.pallas_call(
        _precond_kernel,
        in_specs=[pl.BlockSpec(memory_space=pltpu.VMEM) for _ in range(3)],
        out_specs=pl.BlockSpec(memory_space=pltpu.VMEM),
        out_shape=jax.ShapeDtypeStruct((width, feats), jnp.bfloat16),
        scratch_shapes=[
            pltpu.VMEM((rows, LANES), jnp.float32),
            pltpu.VMEM((rows, LANES), jnp.float32),
            pltpu.VMEM(out_factor.shape, jnp.float32),
        ],
        compiler_params=pltpu.CompilerParams(vmem_limit_bytes=12 << 20),
        name="precond",
    )(*(pltpu.with_memory_space_constraint(x, pltpu.HBM) for x in (out_factor, in_factor, queries)))


def _joined_kernel(*refs):
    *parts, out = refs
    at = 0
    for r in parts:
        out[at : at + PANEL, :] = r[:PANEL, :]
        at += PANEL


def _joined(*parts):
    feats = parts[0].shape[1]
    return pl.pallas_call(
        _joined_kernel,
        in_specs=[pl.BlockSpec(memory_space=pltpu.VMEM) for _ in parts],
        out_specs=pl.BlockSpec(memory_space=pltpu.VMEM),
        out_shape=jax.ShapeDtypeStruct((len(parts) * PANEL, feats), parts[0].dtype),
        compiler_params=pltpu.CompilerParams(vmem_limit_bytes=4 << 20),
        name="joined",
    )(*parts)


def _held(x):
    return pl.pallas_call(
        pltpu.sync_copy,
        in_specs=[pl.BlockSpec(memory_space=pl.ANY)],
        out_specs=pl.BlockSpec(memory_space=pltpu.VMEM),
        out_shape=pltpu.VMEM(x.shape, x.dtype),
        compiler_params=pltpu.CompilerParams(vmem_limit_bytes=1 << 20),
        cost_estimate=pl.CostEstimate(flops=0, bytes_accessed=2 * x.size * 2, transcendentals=0),
        name="held",
    )(x)


def _score_kernel(scale, count, *refs):
    c_ref, o_ref = refs[count], refs[count + 1]
    panels = jnp.concatenate([r[...] for r in refs[:count]], axis=0)
    for i in range(c_ref.shape[0] // CBLK):
        block = slice(i * CBLK, (i + 1) * CBLK)
        part = lax.dot_general(
            panels, c_ref[block, :], (((1,), (1,)), ((), ())), preferred_element_type=jnp.float32
        )
        o_ref[:, block] = (part * scale).astype(o_ref.dtype)


def _score(pieces, flat, scale):
    rows, feats = flat.shape
    n = sum(p.shape[0] for p in pieces)
    return pl.pallas_call(
        functools.partial(_score_kernel, scale, len(pieces)),
        in_specs=[pl.BlockSpec(memory_space=pltpu.VMEM) for _ in range(len(pieces) + 1)],
        out_specs=pl.BlockSpec(memory_space=pltpu.VMEM),
        out_shape=jax.ShapeDtypeStruct((n, rows), jnp.bfloat16),
        compiler_params=pltpu.CompilerParams(vmem_limit_bytes=16 << 20),
        cost_estimate=pl.CostEstimate(
            flops=2 * n * rows * feats, bytes_accessed=2 * (rows * feats + n * feats + n * rows), transcendentals=0
        ),
        name="score",
    )(*pieces, flat)


def _place_kernel(counts, where_ref, *refs):
    out = refs[-1]
    slot = 0
    for ref, count in zip(refs[:-1], counts):
        for i in range(count):
            out[where_ref[slot]] = ref[i * PANEL : (i + 1) * PANEL, :]
            slot += 1


def _place(parts, where):
    counts = [p.shape[0] // PANEL for p in parts]
    rows = parts[0].shape[1]
    return pl.pallas_call(
        functools.partial(_place_kernel, counts),
        in_specs=[pl.BlockSpec(memory_space=pltpu.SMEM)]
        + [pl.BlockSpec(memory_space=pltpu.VMEM) for _ in parts],
        out_specs=pl.BlockSpec(memory_space=pltpu.VMEM),
        out_shape=jax.ShapeDtypeStruct((where.shape[0], PANEL, rows), jnp.bfloat16),
        compiler_params=pltpu.CompilerParams(vmem_limit_bytes=12 << 20),
        name="place",
    )(where, *parts)


def _finish_kernel(scale, count, where_ref, *refs):
    c_ref, o_ref = refs[count], refs[count + 2]
    first = where_ref.shape[0] - count
    panels = jnp.concatenate([r[...] for r in refs[:count]], axis=0)
    for i in range(c_ref.shape[0] // CBLK):
        block = slice(i * CBLK, (i + 1) * CBLK)
        part = lax.dot_general(
            c_ref[block, :], panels, (((1,), (1,)), ((), ())), preferred_element_type=jnp.float32
        )
        part = (part * scale).T.astype(o_ref.dtype)
        for j in range(count):
            o_ref[where_ref[first + j], :, block] = part[j * PANEL : (j + 1) * PANEL, :]


def _finish(pieces, flat, scale, where, early):
    rows, feats = flat.shape
    n = len(pieces) * PANEL
    return pl.pallas_call(
        functools.partial(_finish_kernel, scale, len(pieces)),
        in_specs=[pl.BlockSpec(memory_space=pltpu.SMEM)]
        + [pl.BlockSpec(memory_space=pltpu.VMEM) for _ in range(len(pieces) + 2)],
        out_specs=pl.BlockSpec(memory_space=pltpu.VMEM),
        out_shape=jax.ShapeDtypeStruct(early.shape, early.dtype),
        input_output_aliases={len(pieces) + 2: 0},
        compiler_params=pltpu.CompilerParams(vmem_limit_bytes=16 << 20),
        cost_estimate=pl.CostEstimate(
            flops=2 * n * rows * feats, bytes_accessed=2 * (rows * feats + n * feats + n * rows), transcendentals=0
        ),
        name="finish",
    )(where, *pieces, flat, early)


def _total_kernel(in_ref, o_ref):
    width = in_ref.shape[1]
    for i in range(in_ref.shape[2] // width):
        block = slice(i * width, (i + 1) * width)
        total = in_ref[0, :, block].astype(jnp.float32)
        for g in range(1, in_ref.shape[0]):
            total += in_ref[g, :, block].astype(jnp.float32)
        o_ref[block, :] = total.T


def _total(parts):
    groups, width, rows = parts.shape
    return pl.pallas_call(
        _total_kernel,
        in_specs=[pl.BlockSpec(memory_space=pltpu.VMEM)],
        out_specs=pl.BlockSpec(memory_space=pltpu.VMEM),
        out_shape=jax.ShapeDtypeStruct((rows, width), jnp.float32),
        compiler_params=pltpu.CompilerParams(vmem_limit_bytes=12 << 20),
        name="total",
    )(parts)


def body(candidates, queries, out_factor, in_factor, panel_order):
    cand_rows, layer_count, features = candidates.shape
    width = queries.shape[0]
    groups = lax.axis_size("group")
    scale = 1.0 / (features * layer_count * groups) ** 0.5
    panel = _precond(out_factor[0], in_factor[0], queries.reshape(width, layer_count * features))
    flat = candidates.reshape(cand_rows, layer_count * features)

    me = lax.axis_index("blk")
    z, rest = me // 4, me % 4
    core = me % 2
    up = 1 - 2 * core

    sources = []

    def note(dz, dy):
        sources.append(((z + dz) % NZ) * 4 + (rest ^ (2 * dy)))
        sources.append(((z + dz) % NZ) * 4 + (rest ^ (2 * dy) ^ 1))

    def note_far(dz, dy):
        sources.append(((z + dz) % NZ) * 4 + (rest ^ (2 * dy) ^ 1))
        sources.append(((z + dz) % NZ) * 4 + (rest ^ (2 * dy)))

    note(0, 0)
    note(0, 1)
    for s in range(1, NZ // 2):
        note(-s * up, 0)
        note_far(s * up, 0)
        note(-s * up, 1)
        note_far(s * up, 1)
    for dy in (0, 1):
        sources.append(((z + NZ // 2) % NZ) * 4 + (rest ^ (2 * dy)))
        sources.append(((z + NZ // 2) % NZ) * 4 + (rest ^ (2 * dy) ^ 1))
    source = jnp.stack(sources)
    places = jnp.arange(panel_order.shape[0], dtype=jnp.int32)
    where = jnp.sum(jnp.where(panel_order[None, :] == source[:, None], places[None, :], 0), axis=1).astype(jnp.int32)

    steps = []

    other = _swap_core(panel)
    other, sent = lax.optimization_barrier((other, panel))
    across = _swap_y(sent)
    own, next_to = _along(panel), _along(other)
    flat, where = lax.optimization_barrier((flat, where))
    flat = _held(pltpu.with_memory_space_constraint(flat, pltpu.HBM))
    near = _joined(own, next_to)
    near, across, flat = lax.optimization_barrier((near, across, flat))
    across_other = _swap_core(across)
    far = _along(_joined(across, across_other))
    pieces = [panel, other, across, across_other, near, _swap_core(near), far, _swap_core(far)]
    for s in range(2, NZ // 2):
        near, far = _along(near), _along(far)
        cut = _joined(near)
        near, cut, pieces[0] = lax.optimization_barrier((near, cut, pieces[0]))
        steps.append(_score(pieces, flat, scale))
        if s == NZ // 2 - 1:
            steps[-1], last = lax.optimization_barrier((steps[-1], _along(cut)))
            last, far = lax.optimization_barrier((last, far))
        steps[-1], far = lax.optimization_barrier((steps[-1], far))
        pieces = [near, _swap_core(near), far, _swap_core(far)]
    beyond = _along(_joined(far))
    steps.append(_score(pieces + [last, _swap_core(last)], flat, scale))
    early = _place(steps, where)
    early, beyond = lax.optimization_barrier((early, beyond))
    buffer = _finish([beyond, _swap_core(beyond)], flat, scale, where, early)
    buffer = buffer.reshape(groups, -1, cand_rows)
    parts = lax.all_to_all(buffer, "group", split_axis=0, concat_axis=0, tiled=True)
    return _total(parts)


def solution(mesh):
    in_specs = (
        P("blk", "group", None),
        P("blk", "group", None),
        P("group", None, None),
        P("group", None, None),
        P(),
    )
    out_specs = P("blk", "group")
    return jax.shard_map(body, mesh=mesh, in_specs=in_specs, out_specs=out_specs, check_vma=False)
```

```python
import functools

import jax
import jax.numpy as jnp
from jax import lax
from jax.experimental import pallas as pl
from jax.experimental.pallas import tpu as pltpu
from jax.sharding import PartitionSpec as P

NZ = 8
PANEL = 32
LANES = 128
CBLK = 256


def _route(x, target):
    return lax.ppermute(x, "blk", [(i, target(*divmod(i, 4))) for i in range(NZ * 4)])


def _along(x):
    return _route(x, lambda z, rest: ((z + (1 if rest % 2 == 0 else -1)) % NZ) * 4 + rest)


def _swap_core(x):
    return _route(x, lambda z, rest: z * 4 + (rest ^ 1))


def _swap_y(x):
    return _route(x, lambda z, rest: z * 4 + (rest ^ 2))


def _precond_kernel(a_ref, b_ref, q_ref, o_ref, one_ref, two_ref, left_ref):
    width = q_ref.shape[0]
    tiles = q_ref.shape[1] // LANES
    half = LANES // 2
    zero = jnp.zeros((half, half), jnp.float32)
    b = b_ref[...]
    right = jnp.concatenate(
        [
            jnp.concatenate([b, zero, zero, b], axis=1),
            jnp.concatenate([zero, b, b, zero], axis=1),
        ],
        axis=0,
    )
    rows = jnp.concatenate([q_ref[:, t * LANES : (t + 1) * LANES] for t in range(tiles)], axis=0)
    done = None
    for _ in range(3):
        term = right.astype(jnp.bfloat16)
        right = right - term.astype(jnp.float32)
        part = jnp.dot(rows, term, preferred_element_type=jnp.float32)
        done = part if done is None else done + part
    one_ref[...] = done[:, :LANES]
    two_ref[...] = done[:, LANES:]
    row = lax.broadcasted_iota(jnp.int32, (half, half), 0)
    col = lax.broadcasted_iota(jnp.int32, (half, half), 1)
    unit = jnp.where(col < half // 2, 2 * col, 2 * (col - half // 2) + 1)
    pick = jnp.where(row == unit, 1.0, 0.0).astype(jnp.float32)
    left_ref[...] = jnp.dot(
        a_ref[...], pick, precision=lax.Precision.HIGHEST, preferred_element_type=jnp.float32
    )
    even = left_ref[pl.ds(0, half // 2, stride=2), :]
    odd = left_ref[pl.ds(1, half // 2, stride=2), :]
    odd = jnp.concatenate([odd[:, half // 2 :], odd[:, : half // 2]], axis=1)
    left = jnp.concatenate([even, odd], axis=0)
    lanes = lax.broadcasted_iota(jnp.int32, (tiles, LANES), 1)
    chunk = 8
    for q0 in range(0, width, chunk):
        columns = [
            jnp.concatenate(
                [one_ref[pl.ds(q, tiles, stride=width), :], two_ref[pl.ds(q, tiles, stride=width), :]], axis=0
            )
            for q in range(q0, q0 + chunk)
        ]
        both = jnp.dot(
            left,
            jnp.concatenate(columns, axis=1),
            precision=lax.Precision.HIGHEST,
            preferred_element_type=jnp.float32,
        )
        for i in range(chunk):
            block = both[:, i * LANES : (i + 1) * LANES]
            one_ref[pl.ds(q0 + i, tiles, stride=width), :] = jnp.where(lanes < half, block[:tiles], block[tiles:])
    for t in range(tiles):
        o_ref[:, t * LANES : (t + 1) * LANES] = one_ref[t * width : (t + 1) * width, :].astype(o_ref.dtype)


def _precond(out_factor, in_factor, queries):
    width, feats = queries.shape
    rows = width * feats // LANES
    return pl.pallas_call(
        _precond_kernel,
        in_specs=[pl.BlockSpec(memory_space=pltpu.VMEM) for _ in range(3)],
        out_specs=pl.BlockSpec(memory_space=pltpu.VMEM),
        out_shape=jax.ShapeDtypeStruct((width, feats), jnp.bfloat16),
        scratch_shapes=[
            pltpu.VMEM((rows, LANES), jnp.float32),
            pltpu.VMEM((rows, LANES), jnp.float32),
            pltpu.VMEM(out_factor.shape, jnp.float32),
        ],
        compiler_params=pltpu.CompilerParams(vmem_limit_bytes=12 << 20),
        name="precond",
    )(*(pltpu.with_memory_space_constraint(x, pltpu.HBM) for x in (out_factor, in_factor, queries)))


def _joined_kernel(*refs):
    *parts, out = refs
    at = 0
    for r in parts:
        out[at : at + PANEL, :] = r[:PANEL, :]
        at += PANEL


def _joined(*parts):
    feats = parts[0].shape[1]
    return pl.pallas_call(
        _joined_kernel,
        in_specs=[pl.BlockSpec(memory_space=pltpu.VMEM) for _ in parts],
        out_specs=pl.BlockSpec(memory_space=pltpu.VMEM),
        out_shape=jax.ShapeDtypeStruct((len(parts) * PANEL, feats), parts[0].dtype),
        compiler_params=pltpu.CompilerParams(vmem_limit_bytes=4 << 20),
        name="joined",
    )(*parts)


def _held(x):
    return pl.pallas_call(
        pltpu.sync_copy,
        in_specs=[pl.BlockSpec(memory_space=pl.ANY)],
        out_specs=pl.BlockSpec(memory_space=pltpu.VMEM),
        out_shape=pltpu.VMEM(x.shape, x.dtype),
        compiler_params=pltpu.CompilerParams(vmem_limit_bytes=1 << 20),
        cost_estimate=pl.CostEstimate(flops=0, bytes_accessed=2 * x.size * 2, transcendentals=0),
        name="held",
    )(x)


def _score_kernel(scale, count, *refs):
    c_ref, o_ref = refs[count], refs[count + 1]
    panels = jnp.concatenate([r[...] for r in refs[:count]], axis=0)
    for i in range(c_ref.shape[0] // CBLK):
        block = slice(i * CBLK, (i + 1) * CBLK)
        part = lax.dot_general(
            panels, c_ref[block, :], (((1,), (1,)), ((), ())), preferred_element_type=jnp.float32
        )
        o_ref[:, block] = (part * scale).astype(o_ref.dtype)


def _score(pieces, flat, scale):
    rows, feats = flat.shape
    n = sum(p.shape[0] for p in pieces)
    return pl.pallas_call(
        functools.partial(_score_kernel, scale, len(pieces)),
        in_specs=[pl.BlockSpec(memory_space=pltpu.VMEM) for _ in range(len(pieces) + 1)],
        out_specs=pl.BlockSpec(memory_space=pltpu.VMEM),
        out_shape=jax.ShapeDtypeStruct((n, rows), jnp.bfloat16),
        compiler_params=pltpu.CompilerParams(vmem_limit_bytes=16 << 20),
        cost_estimate=pl.CostEstimate(
            flops=2 * n * rows * feats, bytes_accessed=2 * (rows * feats + n * feats + n * rows), transcendentals=0
        ),
        name="score",
    )(*pieces, flat)


def _place_kernel(counts, where_ref, *refs):
    out = refs[-1]
    slot = 0
    for ref, count in zip(refs[:-1], counts):
        for i in range(count):
            out[where_ref[slot]] = ref[i * PANEL : (i + 1) * PANEL, :]
            slot += 1


def _place(parts, where):
    counts = [p.shape[0] // PANEL for p in parts]
    rows = parts[0].shape[1]
    return pl.pallas_call(
        functools.partial(_place_kernel, counts),
        in_specs=[pl.BlockSpec(memory_space=pltpu.SMEM)]
        + [pl.BlockSpec(memory_space=pltpu.VMEM) for _ in parts],
        out_specs=pl.BlockSpec(memory_space=pltpu.VMEM),
        out_shape=jax.ShapeDtypeStruct((where.shape[0], PANEL, rows), jnp.bfloat16),
        compiler_params=pltpu.CompilerParams(vmem_limit_bytes=12 << 20),
        name="place",
    )(where, *parts)


def _finish_kernel(scale, count, where_ref, *refs):
    c_ref, o_ref = refs[count], refs[count + 2]
    first = where_ref.shape[0] - count
    panels = jnp.concatenate([r[...] for r in refs[:count]], axis=0)
    for i in range(c_ref.shape[0] // CBLK):
        block = slice(i * CBLK, (i + 1) * CBLK)
        part = lax.dot_general(
            c_ref[block, :], panels, (((1,), (1,)), ((), ())), preferred_element_type=jnp.float32
        )
        part = (part * scale).T.astype(o_ref.dtype)
        for j in range(count):
            o_ref[where_ref[first + j], :, block] = part[j * PANEL : (j + 1) * PANEL, :]


def _finish(pieces, flat, scale, where, early):
    rows, feats = flat.shape
    n = len(pieces) * PANEL
    return pl.pallas_call(
        functools.partial(_finish_kernel, scale, len(pieces)),
        in_specs=[pl.BlockSpec(memory_space=pltpu.SMEM)]
        + [pl.BlockSpec(memory_space=pltpu.VMEM) for _ in range(len(pieces) + 2)],
        out_specs=pl.BlockSpec(memory_space=pltpu.VMEM),
        out_shape=jax.ShapeDtypeStruct(early.shape, early.dtype),
        input_output_aliases={len(pieces) + 2: 0},
        compiler_params=pltpu.CompilerParams(vmem_limit_bytes=16 << 20),
        cost_estimate=pl.CostEstimate(
            flops=2 * n * rows * feats, bytes_accessed=2 * (rows * feats + n * feats + n * rows), transcendentals=0
        ),
        name="finish",
    )(where, *pieces, flat, early)


def _total_kernel(in_ref, o_ref):
    width = in_ref.shape[1]
    for i in range(in_ref.shape[2] // width):
        block = slice(i * width, (i + 1) * width)
        total = in_ref[0, :, block].astype(jnp.float32)
        for g in range(1, in_ref.shape[0]):
            total += in_ref[g, :, block].astype(jnp.float32)
        o_ref[block, :] = total.T


def _total(parts):
    groups, width, rows = parts.shape
    return pl.pallas_call(
        _total_kernel,
        in_specs=[pl.BlockSpec(memory_space=pltpu.VMEM)],
        out_specs=pl.BlockSpec(memory_space=pltpu.VMEM),
        out_shape=jax.ShapeDtypeStruct((rows, width), jnp.float32),
        compiler_params=pltpu.CompilerParams(vmem_limit_bytes=12 << 20),
        name="total",
    )(parts)


def body(candidates, queries, out_factor, in_factor, panel_order):
    cand_rows, layer_count, features = candidates.shape
    width = queries.shape[0]
    groups = lax.axis_size("group")
    scale = 1.0 / (features * layer_count * groups) ** 0.5
    panel = _precond(out_factor[0], in_factor[0], queries.reshape(width, layer_count * features))
    flat = candidates.reshape(cand_rows, layer_count * features)

    me = lax.axis_index("blk")
    z, rest = me // 4, me % 4
    core = me % 2
    up = 1 - 2 * core

    sources = []

    def note(dz, dy):
        sources.append(((z + dz) % NZ) * 4 + (rest ^ (2 * dy)))
        sources.append(((z + dz) % NZ) * 4 + (rest ^ (2 * dy) ^ 1))

    def note_far(dz, dy):
        sources.append(((z + dz) % NZ) * 4 + (rest ^ (2 * dy) ^ 1))
        sources.append(((z + dz) % NZ) * 4 + (rest ^ (2 * dy)))

    note(0, 0)
    note(0, 1)
    for s in range(1, NZ // 2):
        note(-s * up, 0)
        note_far(s * up, 0)
        note(-s * up, 1)
        note_far(s * up, 1)
    for dy in (0, 1):
        sources.append(((z + NZ // 2) % NZ) * 4 + (rest ^ (2 * dy)))
        sources.append(((z + NZ // 2) % NZ) * 4 + (rest ^ (2 * dy) ^ 1))
    source = jnp.stack(sources)
    places = jnp.arange(panel_order.shape[0], dtype=jnp.int32)
    where = jnp.sum(jnp.where(panel_order[None, :] == source[:, None], places[None, :], 0), axis=1).astype(jnp.int32)

    steps = []

    other = _swap_core(panel)
    other, sent = lax.optimization_barrier((other, panel))
    across = _swap_y(sent)
    own, next_to = _along(panel), _along(other)
    flat, where = lax.optimization_barrier((flat, where))
    flat = _held(pltpu.with_memory_space_constraint(flat, pltpu.HBM))
    near = _joined(own, next_to)
    near, across, flat = lax.optimization_barrier((near, across, flat))
    across_other = _swap_core(across)
    far = _joined(_along(across), _along(across_other))
    pieces = [panel, other, across, across_other, near, _swap_core(near), far, _swap_core(far)]
    for s in range(2, NZ // 2):
        near, far = _along(near), _along(far)
        cut = _joined(near)
        near, cut, pieces[0] = lax.optimization_barrier((near, cut, pieces[0]))
        steps.append(_score(pieces, flat, scale))
        if s == NZ // 2 - 1:
            steps[-1], last = lax.optimization_barrier((steps[-1], _along(cut)))
            last, far = lax.optimization_barrier((last, far))
        steps[-1], far = lax.optimization_barrier((steps[-1], far))
        pieces = [near, _swap_core(near), far, _swap_core(far)]
    beyond = _along(_joined(far))
    steps.append(_score(pieces + [last, _swap_core(last)], flat, scale))
    early = _place(steps, where)
    early, beyond = lax.optimization_barrier((early, beyond))
    buffer = _finish([beyond, _swap_core(beyond)], flat, scale, where, early)
    buffer = buffer.reshape(groups, -1, cand_rows)
    parts = lax.all_to_all(buffer, "group", split_axis=0, concat_axis=0, tiled=True)
    return _total(parts)


def solution(mesh):
    in_specs = (
        P("blk", "group", None),
        P("blk", "group", None),
        P("group", None, None),
        P("group", None, None),
        P(),
    )
    out_specs = P("blk", "group")
    return jax.shard_map(body, mesh=mesh, in_specs=in_specs, out_specs=out_specs, check_vma=False)
```

```python
import functools

import jax
import jax.numpy as jnp
from jax import lax
from jax.experimental import pallas as pl
from jax.experimental.pallas import tpu as pltpu
from jax.sharding import PartitionSpec as P

NZ = 8
PANEL = 32
LANES = 128
CBLK = 256


def _route(x, target):
    return lax.ppermute(x, "blk", [(i, target(*divmod(i, 4))) for i in range(NZ * 4)])


def _along(x):
    return _route(x, lambda z, rest: ((z + (1 if rest % 2 == 0 else -1)) % NZ) * 4 + rest)


def _swap_core(x):
    return _route(x, lambda z, rest: z * 4 + (rest ^ 1))


def _swap_y(x):
    return _route(x, lambda z, rest: z * 4 + (rest ^ 2))


def _precond_kernel(a_ref, b_ref, q_ref, o_ref, one_ref, two_ref, left_ref):
    width = q_ref.shape[0]
    tiles = q_ref.shape[1] // LANES
    half = LANES // 2
    zero = jnp.zeros((half, half), jnp.float32)
    b = b_ref[...]
    right = jnp.concatenate(
        [
            jnp.concatenate([b, zero, zero, b], axis=1),
            jnp.concatenate([zero, b, b, zero], axis=1),
        ],
        axis=0,
    )
    rows = jnp.concatenate([q_ref[:, t * LANES : (t + 1) * LANES] for t in range(tiles)], axis=0)
    done = None
    for _ in range(3):
        term = right.astype(jnp.bfloat16)
        right = right - term.astype(jnp.float32)
        part = jnp.dot(rows, term, preferred_element_type=jnp.float32)
        done = part if done is None else done + part
    one_ref[...] = done[:, :LANES]
    two_ref[...] = done[:, LANES:]
    row = lax.broadcasted_iota(jnp.int32, (half, half), 0)
    col = lax.broadcasted_iota(jnp.int32, (half, half), 1)
    unit = jnp.where(col < half // 2, 2 * col, 2 * (col - half // 2) + 1)
    pick = jnp.where(row == unit, 1.0, 0.0).astype(jnp.float32)
    left_ref[...] = jnp.dot(
        a_ref[...], pick, precision=lax.Precision.HIGHEST, preferred_element_type=jnp.float32
    )
    even = left_ref[pl.ds(0, half // 2, stride=2), :]
    odd = left_ref[pl.ds(1, half // 2, stride=2), :]
    odd = jnp.concatenate([odd[:, half // 2 :], odd[:, : half // 2]], axis=1)
    left = jnp.concatenate([even, odd], axis=0)
    lanes = lax.broadcasted_iota(jnp.int32, (tiles, LANES), 1)
    chunk = 8
    for q0 in range(0, width, chunk):
        columns = [
            jnp.concatenate(
                [one_ref[pl.ds(q, tiles, stride=width), :], two_ref[pl.ds(q, tiles, stride=width), :]], axis=0
            )
            for q in range(q0, q0 + chunk)
        ]
        both = jnp.dot(
            left,
            jnp.concatenate(columns, axis=1),
            precision=lax.Precision.HIGHEST,
            preferred_element_type=jnp.float32,
        )
        for i in range(chunk):
            block = both[:, i * LANES : (i + 1) * LANES]
            one_ref[pl.ds(q0 + i, tiles, stride=width), :] = jnp.where(lanes < half, block[:tiles], block[tiles:])
    for t in range(tiles):
        o_ref[:, t * LANES : (t + 1) * LANES] = one_ref[t * width : (t + 1) * width, :].astype(o_ref.dtype)


def _precond(out_factor, in_factor, queries):
    width, feats = queries.shape
    rows = width * feats // LANES
    return pl.pallas_call(
        _precond_kernel,
        in_specs=[pl.BlockSpec(memory_space=pltpu.VMEM) for _ in range(3)],
        out_specs=pl.BlockSpec(memory_space=pltpu.VMEM),
        out_shape=jax.ShapeDtypeStruct((width, feats), jnp.bfloat16),
        scratch_shapes=[
            pltpu.VMEM((rows, LANES), jnp.float32),
            pltpu.VMEM((rows, LANES), jnp.float32),
            pltpu.VMEM(out_factor.shape, jnp.float32),
        ],
        compiler_params=pltpu.CompilerParams(vmem_limit_bytes=12 << 20),
        name="precond",
    )(*(pltpu.with_memory_space_constraint(x, pltpu.HBM) for x in (out_factor, in_factor, queries)))


def _joined_kernel(*refs):
    *parts, out = refs
    at = 0
    for r in parts:
        out[at : at + PANEL, :] = r[:PANEL, :]
        at += PANEL


def _joined(*parts):
    feats = parts[0].shape[1]
    return pl.pallas_call(
        _joined_kernel,
        in_specs=[pl.BlockSpec(memory_space=pltpu.VMEM) for _ in parts],
        out_specs=pl.BlockSpec(memory_space=pltpu.VMEM),
        out_shape=jax.ShapeDtypeStruct((len(parts) * PANEL, feats), parts[0].dtype),
        compiler_params=pltpu.CompilerParams(vmem_limit_bytes=4 << 20),
        name="joined",
    )(*parts)


def _held(x):
    return pl.pallas_call(
        pltpu.sync_copy,
        in_specs=[pl.BlockSpec(memory_space=pl.ANY)],
        out_specs=pl.BlockSpec(memory_space=pltpu.VMEM),
        out_shape=pltpu.VMEM(x.shape, x.dtype),
        compiler_params=pltpu.CompilerParams(vmem_limit_bytes=1 << 20),
        cost_estimate=pl.CostEstimate(flops=0, bytes_accessed=2 * x.size * 2, transcendentals=0),
        name="held",
    )(x)


def _score_kernel(scale, count, *refs):
    c_ref, o_ref = refs[count], refs[count + 1]
    panels = jnp.concatenate([r[...] for r in refs[:count]], axis=0)
    for i in range(c_ref.shape[0] // CBLK):
        block = slice(i * CBLK, (i + 1) * CBLK)
        part = lax.dot_general(
            panels, c_ref[block, :], (((1,), (1,)), ((), ())), preferred_element_type=jnp.float32
        )
        o_ref[:, block] = (part * scale).astype(o_ref.dtype)


def _score(pieces, flat, scale):
    rows, feats = flat.shape
    n = sum(p.shape[0] for p in pieces)
    return pl.pallas_call(
        functools.partial(_score_kernel, scale, len(pieces)),
        in_specs=[pl.BlockSpec(memory_space=pltpu.VMEM) for _ in range(len(pieces) + 1)],
        out_specs=pl.BlockSpec(memory_space=pltpu.VMEM),
        out_shape=jax.ShapeDtypeStruct((n, rows), jnp.bfloat16),
        compiler_params=pltpu.CompilerParams(vmem_limit_bytes=16 << 20),
        cost_estimate=pl.CostEstimate(
            flops=2 * n * rows * feats, bytes_accessed=2 * (rows * feats + n * feats + n * rows), transcendentals=0
        ),
        name="score",
    )(*pieces, flat)


def _place_kernel(counts, where_ref, *refs):
    out = refs[-1]
    slot = 0
    for ref, count in zip(refs[:-1], counts):
        for i in range(count):
            out[where_ref[slot]] = ref[i * PANEL : (i + 1) * PANEL, :]
            slot += 1


def _place(parts, where):
    counts = [p.shape[0] // PANEL for p in parts]
    rows = parts[0].shape[1]
    return pl.pallas_call(
        functools.partial(_place_kernel, counts),
        in_specs=[pl.BlockSpec(memory_space=pltpu.SMEM)]
        + [pl.BlockSpec(memory_space=pltpu.VMEM) for _ in parts],
        out_specs=pl.BlockSpec(memory_space=pltpu.VMEM),
        out_shape=jax.ShapeDtypeStruct((where.shape[0], PANEL, rows), jnp.bfloat16),
        compiler_params=pltpu.CompilerParams(vmem_limit_bytes=12 << 20),
        name="place",
    )(where, *parts)


def _finish_kernel(scale, count, where_ref, *refs):
    c_ref, o_ref = refs[count], refs[count + 2]
    first = where_ref.shape[0] - count
    panels = jnp.concatenate([r[...] for r in refs[:count]], axis=0)
    for i in range(c_ref.shape[0] // CBLK):
        block = slice(i * CBLK, (i + 1) * CBLK)
        part = lax.dot_general(
            c_ref[block, :], panels, (((1,), (1,)), ((), ())), preferred_element_type=jnp.float32
        )
        part = (part * scale).T.astype(o_ref.dtype)
        for j in range(count):
            o_ref[where_ref[first + j], :, block] = part[j * PANEL : (j + 1) * PANEL, :]


def _finish(pieces, flat, scale, where, early):
    rows, feats = flat.shape
    n = len(pieces) * PANEL
    return pl.pallas_call(
        functools.partial(_finish_kernel, scale, len(pieces)),
        in_specs=[pl.BlockSpec(memory_space=pltpu.SMEM)]
        + [pl.BlockSpec(memory_space=pltpu.VMEM) for _ in range(len(pieces) + 2)],
        out_specs=pl.BlockSpec(memory_space=pltpu.VMEM),
        out_shape=jax.ShapeDtypeStruct(early.shape, early.dtype),
        input_output_aliases={len(pieces) + 2: 0},
        compiler_params=pltpu.CompilerParams(vmem_limit_bytes=16 << 20),
        cost_estimate=pl.CostEstimate(
            flops=2 * n * rows * feats, bytes_accessed=2 * (rows * feats + n * feats + n * rows), transcendentals=0
        ),
        name="finish",
    )(where, *pieces, flat, early)


def _total_kernel(in_ref, o_ref):
    width = in_ref.shape[1]
    for i in range(in_ref.shape[2] // width):
        block = slice(i * width, (i + 1) * width)
        total = in_ref[0, :, block].astype(jnp.float32)
        for g in range(1, in_ref.shape[0]):
            total += in_ref[g, :, block].astype(jnp.float32)
        o_ref[block, :] = total.T


def _total(parts):
    groups, width, rows = parts.shape
    return pl.pallas_call(
        _total_kernel,
        in_specs=[pl.BlockSpec(memory_space=pltpu.VMEM)],
        out_specs=pl.BlockSpec(memory_space=pltpu.VMEM),
        out_shape=jax.ShapeDtypeStruct((rows, width), jnp.float32),
        compiler_params=pltpu.CompilerParams(vmem_limit_bytes=12 << 20),
        name="total",
    )(parts)


def body(candidates, queries, out_factor, in_factor, panel_order):
    cand_rows, layer_count, features = candidates.shape
    width = queries.shape[0]
    groups = lax.axis_size("group")
    scale = 1.0 / (features * layer_count * groups) ** 0.5
    panel = _precond(out_factor[0], in_factor[0], queries.reshape(width, layer_count * features))
    flat = candidates.reshape(cand_rows, layer_count * features)

    me = lax.axis_index("blk")
    z, rest = me // 4, me % 4
    core = me % 2
    up = 1 - 2 * core

    sources = []

    def note(dz, dy):
        sources.append(((z + dz) % NZ) * 4 + (rest ^ (2 * dy)))
        sources.append(((z + dz) % NZ) * 4 + (rest ^ (2 * dy) ^ 1))

    def note_far(dz, dy):
        sources.append(((z + dz) % NZ) * 4 + (rest ^ (2 * dy) ^ 1))
        sources.append(((z + dz) % NZ) * 4 + (rest ^ (2 * dy)))

    note(0, 0)
    note(0, 1)
    for s in range(1, NZ // 2):
        note(-s * up, 0)
        note_far(s * up, 0)
        note(-s * up, 1)
        note_far(s * up, 1)
    for dy in (0, 1):
        sources.append(((z + NZ // 2) % NZ) * 4 + (rest ^ (2 * dy)))
        sources.append(((z + NZ // 2) % NZ) * 4 + (rest ^ (2 * dy) ^ 1))
    source = jnp.stack(sources)
    places = jnp.arange(panel_order.shape[0], dtype=jnp.int32)
    where = jnp.sum(jnp.where(panel_order[None, :] == source[:, None], places[None, :], 0), axis=1).astype(jnp.int32)

    steps = []

    other = _swap_core(panel)
    other, sent = lax.optimization_barrier((other, panel))
    across = _swap_y(sent)
    own, next_to = _along(panel), _along(other)
    flat, where = lax.optimization_barrier((flat, where))
    flat = _held(pltpu.with_memory_space_constraint(flat, pltpu.HBM))
    near = _joined(own, next_to)
    near, across, flat = lax.optimization_barrier((near, across, flat))
    across_other = _swap_core(across)
    halves = _along(across), _along(across_other)
    far = _joined(*halves)
    pieces = [panel, other, across, across_other, near, _swap_core(near), far, _swap_core(far)]
    for s in range(2, NZ // 2):
        near, far = _along(near), _joined(*map(_along, halves)) if s == 2 else _along(far)
        cut = _joined(near)
        near, cut, pieces[0] = lax.optimization_barrier((near, cut, pieces[0]))
        steps.append(_score(pieces, flat, scale))
        if s == NZ // 2 - 1:
            steps[-1], last = lax.optimization_barrier((steps[-1], _along(cut)))
            last, far = lax.optimization_barrier((last, far))
        steps[-1], far = lax.optimization_barrier((steps[-1], far))
        pieces = [near, _swap_core(near), far, _swap_core(far)]
    beyond = _along(_joined(far))
    steps.append(_score(pieces + [last, _swap_core(last)], flat, scale))
    early = _place(steps, where)
    early, beyond = lax.optimization_barrier((early, beyond))
    buffer = _finish([beyond, _swap_core(beyond)], flat, scale, where, early)
    buffer = buffer.reshape(groups, -1, cand_rows)
    parts = lax.all_to_all(buffer, "group", split_axis=0, concat_axis=0, tiled=True)
    return _total(parts)


def solution(mesh):
    in_specs = (
        P("blk", "group", None),
        P("blk", "group", None),
        P("group", None, None),
        P("group", None, None),
        P(),
    )
    out_specs = P("blk", "group")
    return jax.shard_map(body, mesh=mesh, in_specs=in_specs, out_specs=out_specs, check_vma=False)
```
